128 devices in a mesh: wide: 32 (over y, x, core), cross: 4 (over z).
Axes of the slice: x: 4, y: 4, z: 4, core: 2. Of those that a mesh axis runs over, the one named last changes fastest.
Arguments:
- rhs: float32 [3, 128, 32, 257], P(None, 'wide', 'cross'), may hold values from -6 to 6
- start: float32 [3, 128, 32, 257], P(None, 'wide', 'cross'), may hold values from -6 to 6
- stiffness: float32 [32, 8, 64], P('wide', 'cross'), may hold values from 1 to 10
- fibre_index: int32 [32, 8, 64], P('wide', 'cross'), may hold values from 0 to 63
Outputs:
- solution: float32 [3, 128, 32, 257], P(None, 'wide', 'cross')
- correction: float32 [3, 32, 8, 65], P(None, 'wide', 'cross')
The draws below stay inside these ranges and needn't reach their ends.
All inputs are finite; a program needn't handle non-finite values.
Results may differ from the reference program's by a relative error of at most 0.0003.
Values sent between devices are 32-bit elements; how exact they have to be, the bound alone decides.
A program may use at most 128 MiB of HBM per device.

```python
import math
import jax
import jax.numpy as jnp
import numpy as np
from jax import lax

EZ = 64
NFIB = 64
NEX = 32
NEY = 8
NX = 128
NY = 32
NZ = 257


def place_ends(values, key, least, top_value):
    extent = values.shape
    spot = [jax.random.randint(jax.random.fold_in(key, axis), (), 0, extent[axis]) for axis in range(len(extent))]
    values = values.at[tuple(spot)].set(least)
    longest = extent.index(max(extent))
    spot[longest] = (spot[longest] + 1) % extent[longest]
    return values.at[tuple(spot)].set(top_value)


def block_scale(stream_key, extent, pieces, least, high):
    factor_of, own = 1.0, jax.random.fold_in(stream_key, 6)
    for dim, shards_of in pieces:
        draws = jnp.exp(jax.random.uniform(jax.random.fold_in(own, dim), (shards_of,), jnp.float32, least / len(pieces), high / len(pieces)))
        factor_of = factor_of * jnp.repeat(draws, extent[dim] // shards_of).reshape([-1 if axis == dim else 1 for axis in range(len(extent))])
    return factor_of


def noise(rng, dims, spread, reach, split=(), held_as=jnp.bfloat16):
    values = spread * jax.random.normal(rng, dims, jnp.float32)
    if split:
        values = values * block_scale(rng, dims, split, -0.22, 0.18)
    return jnp.clip(values, -reach, reach).astype(held_as)


def setup_inputs(seed: int = 0) -> dict:
    streams_of = jax.random.split(jax.random.key(seed), 5)
    return {
        "rhs": noise(streams_of[0], (3, NX, NY, NZ), 1.0, 6.0, ((1, 32), (2, 4)), jnp.float32),
        "start": noise(streams_of[1], (3, NX, NY, NZ), 0.5, 6.0, ((1, 32), (2, 4)), jnp.float32),
        "stiffness": jnp.clip(jnp.exp(math.log(10.0) - 2.3025851 * jax.random.uniform(streams_of[2], (NEX, NEY, EZ), jnp.float32) ** block_scale(streams_of[2], (NEX, NEY, EZ), ((0, 32), (1, 4)), -0.2, 0.2)), 1.0, 10.0),
        "fibre_index": place_ends(jax.random.randint(streams_of[3], (NEX, NEY, EZ), 0, NFIB), jax.random.fold_in(streams_of[3], 1), 0, NFIB - 1).astype(jnp.int32),
    }


LAMBDA_COEF = 2.0
SHEAR_CROSS = 1.0
SHEAR_ALONG = 3.0
FIBRE_COEF = 20.0
MASS_COEF = 0.02
FINE_RATIO = 10.0
COARSE_RATIO = 30.0

def gll_points():
    root = math.sqrt(3.0 / 7.0)
    points = (np.array([-1.0, -root, 0.0, root, 1.0]) + 1.0) / 2.0
    weights = np.array([0.1, 49.0 / 90.0, 32.0 / 45.0, 49.0 / 90.0, 0.1]) / 2.0
    return (points, weights)

def lagrange_slopes(points, where):
    count = len(points)
    table = np.zeros((len(where), count))
    for i, spot in enumerate(where):
        for j in range(count):
            total = 0.0
            for k in range(count):
                if k == j:
                    continue
                term = 1.0 / (points[j] - points[k])
                for m in range(count):
                    if m != j and m != k:
                        term = term * (spot - points[m]) / (points[j] - points[m])
                total = total + term
            table[i, j] = total
    return table

def element_tables(degree):
    if degree == 4:
        points, weights = gll_points()
        basis = np.eye(5)
        slopes = lagrange_slopes(points, points)
    else:
        gauss = np.array([0.5 - 0.5 / math.sqrt(3.0), 0.5 + 0.5 / math.sqrt(3.0)])
        basis = np.stack([1.0 - gauss, gauss], 1)
        slopes = np.array([[-1.0, 1.0], [-1.0, 1.0]])
        weights = np.array([0.5, 0.5])
    cube = weights[:, None, None] * weights[None, :, None] * weights[None, None, :]
    return (jnp.asarray(basis, dtype=jnp.float32), jnp.asarray(slopes, dtype=jnp.float32), jnp.asarray(cube, dtype=jnp.float32))

def prolong_table(count, rows):
    points, weights = gll_points()
    table = np.zeros((rows, count + 1))
    for r in range(rows):
        elem, i = divmod(r, 4)
        if elem == count:
            table[r, count] = 1.0
        else:
            table[r, elem] = 1.0 - points[i]
            table[r, elem + 1] = points[i]
    return jnp.asarray(table, dtype=jnp.float32)

def fibre_vectors(index):
    angle = index.astype(jnp.float32) * (2.0 * math.pi / NFIB)
    tilt = 0.4 * jnp.sin(3.0 * angle)
    fibre = jnp.stack([jnp.cos(angle) * jnp.cos(tilt), jnp.sin(angle) * jnp.cos(tilt), jnp.sin(tilt)])
    return fibre.reshape(3, -1)

def contract(field, table, axis):
    forms = ('qa,abce->qbce', 'qb,abce->aqce', 'qc,abce->abqe')
    return jnp.einsum(forms[axis], table, field, precision=lax.Precision.HIGHEST)

def element_apply(local, basis, slopes, cube, stiff, fibre):
    gradient = [[None] * 3 for _ in range(3)]
    values = []
    for c in range(3):
        for d in range(3):
            field = local[c]
            for a in range(3):
                field = contract(field, slopes if a == d else basis, a)
            gradient[c][d] = field
        field = local[c]
        for a in range(3):
            field = contract(field, basis, a)
        values.append(field)
    strain = [[0.5 * (gradient[i][j] + gradient[j][i]) for j in range(3)] for i in range(3)]
    trace_sum = strain[0][0] + strain[1][1] + strain[2][2]
    along = [strain[i][0] * fibre[0] + strain[i][1] * fibre[1] + strain[i][2] * fibre[2] for i in range(3)]
    stretch = fibre[0] * along[0] + fibre[1] * along[1] + fibre[2] * along[2]
    weighted = cube[..., None] * stiff
    mass_weight = MASS_COEF * cube[..., None]
    result = []
    for c in range(3):
        field = values[c] * mass_weight
        for a in range(3):
            field = contract(field, basis.T, a)
        total = field
        for d in range(3):
            stress = 2.0 * SHEAR_CROSS * strain[c][d]
            stress = stress + 2.0 * (SHEAR_ALONG - SHEAR_CROSS) * (fibre[c] * along[d] + along[c] * fibre[d])
            stress = stress + FIBRE_COEF * stretch * fibre[c] * fibre[d]
            if c == d:
                stress = stress + LAMBDA_COEF * trace_sum
            field = stress * weighted
            for a in range(3):
                field = contract(field, (slopes if a == d else basis).T, a)
            total = total + field
        result.append(total)
    return jnp.stack(result)

def to_local(field, degree):
    count = (field.shape[-1] - 1) // degree
    first = field[..., :-1].reshape(field.shape[:-1] + (count, degree))
    last = field[..., degree::degree]
    return jnp.concatenate([first, last[..., None]], -1)

def from_local(field, degree):
    count = field.shape[-2]
    lead = field.shape[:-2]
    main = field[..., :degree].reshape(lead + (count * degree,))
    tail = jnp.concatenate([jnp.zeros(lead + (count, degree - 1), field.dtype), field[..., degree:]], -1)
    tail = tail.reshape(lead + (count * degree,))
    spare = [(0, 0)] * len(lead)
    return jnp.pad(main, spare + [(0, 1)]) + jnp.pad(tail, spare + [(1, 0)])

def apply_operator(extended, degree, stiff, fibre):
    basis, slopes, cube = element_tables(degree)
    nodes = degree + 1
    view = to_local(extended, degree)
    view = to_local(jnp.moveaxis(view, 2, -1), degree)
    view = to_local(jnp.moveaxis(view, 1, -1), degree)
    counts = (view.shape[5], view.shape[3], view.shape[1])
    view = jnp.transpose(view, (0, 6, 4, 2, 5, 3, 1)).reshape(3, nodes, nodes, nodes, -1)
    result = element_apply(view, basis, slopes, cube, stiff, fibre)
    result = result.reshape((3, nodes, nodes, nodes) + counts)
    result = jnp.transpose(result, (0, 6, 3, 5, 2, 4, 1))
    result = jnp.moveaxis(from_local(result, degree), -1, 1)
    result = jnp.moveaxis(from_local(result, degree), -1, 2)
    return from_local(result, degree)

def closed_apply(field, degree, stiff, fibre):
    extended = jnp.pad(field, ((0, 0), (0, 1), (0, 1), (0, 0)))
    return apply_operator(extended, degree, stiff, fibre)[:, :-1, :-1]

def apply_axis(field, table, axis):
    forms = ('ra,cabd->crbd', 'rb,cabd->card', 'rd,cabd->cabr')
    return jnp.einsum(forms[axis], table, field, precision=lax.Precision.HIGHEST)

def power_estimate(start_vec, operator, total):
    vector = start_vec / jnp.sqrt(total(start_vec) + 1e-06)
    square = None
    for k in range(3):
        image = operator(vector)
        square = total(image)
        vector = image / jnp.sqrt(square + 1e-06)
    return jnp.sqrt(square + 1e-06)

def chebyshev(approx, residual, largest, ratio_value, operator, keep):
    upper = 1.1 * largest
    lower = upper / ratio_value
    centre = 0.5 * (upper + lower)
    radius = 0.5 * (upper - lower)
    spread_ratio = centre / radius
    weight_old = 1.0 / spread_ratio
    step = residual / centre
    for k in range(4):
        approx = approx + step
        if k < 3 or keep:
            residual = residual - operator(step)
        if k < 3:
            weight_new = 1.0 / (2.0 * spread_ratio - weight_old)
            step = weight_new * weight_old * step + 2.0 * weight_new / radius * residual
            weight_old = weight_new
    return (approx, residual)

def reference(rhs, start, stiffness, fibre_index):
    stiff = stiffness.reshape(-1)
    fibre = fibre_vectors(fibre_index)

    def fine_op(field):
        return closed_apply(field, 4, stiff, fibre)

    def coarse_op(field):
        return closed_apply(field, 1, stiff, fibre)

    def total(field):
        return jnp.sum(field * field)
    table_x = prolong_table(NEX, NX)
    table_y = prolong_table(NEY, NY)
    table_z = prolong_table(EZ, NZ)
    residual = rhs - fine_op(start)
    largest = power_estimate(residual, fine_op, total)
    approx, residual = chebyshev(start, residual, largest, FINE_RATIO, fine_op, True)
    coarse_rhs = apply_axis(apply_axis(apply_axis(residual, table_z.T, 2), table_y.T, 1), table_x.T, 0)
    coarse_rhs = coarse_rhs[:, :-1, :-1]
    coarse_largest = power_estimate(coarse_rhs, coarse_op, total)
    correction, unused = chebyshev(jnp.zeros_like(coarse_rhs), coarse_rhs, coarse_largest, COARSE_RATIO, coarse_op, False)
    padded = jnp.pad(correction, ((0, 0), (0, 1), (0, 1), (0, 0)))
    approx = approx + apply_axis(apply_axis(apply_axis(padded, table_x, 0), table_y, 1), table_z, 2)
    residual = rhs - fine_op(approx)
    approx, unused = chebyshev(approx, residual, largest, FINE_RATIO, fine_op, False)
    return (approx, correction)
```

```python
import functools
import math

import jax
import jax.numpy as jnp
import numpy as np
from jax import lax
from jax.experimental import pallas as pl
from jax.experimental.pallas import tpu as pltpu
from jax.sharding import PartitionSpec as P

NFIB = 64
LAMBDA_COEF = 2.0
SHEAR_CROSS = 1.0
SHEAR_ALONG = 3.0
FIBRE_COEF = 20.0
MASS_COEF = 0.02
FINE_RATIO = 10.0
COARSE_RATIO = 30.0

MESH = pl.DeviceIdType.MESH
HIGHEST = lax.Precision.HIGHEST
LANES = 128
PER = 200
ROWS = 3 * PER
HELD = ROWS + 56
NEIGHBOURS = ((-1, 0), (1, 0), (0, -1), (0, 1), (-1, -1), (-1, 1), (1, -1), (1, 1))
FACE_X, FACE_Y, EDGE = 80, 64, 24
SIZES = (FACE_X, FACE_X, FACE_Y, FACE_Y, EDGE, EDGE, EDGE, EDGE)


def gll_points():
    root = math.sqrt(3.0 / 7.0)
    points = (np.array([-1.0, -root, 0.0, root, 1.0]) + 1.0) / 2.0
    weights = np.array([0.1, 49.0 / 90.0, 32.0 / 45.0, 49.0 / 90.0, 0.1]) / 2.0
    return (points, weights)


def lagrange_slopes(points, where):
    count = len(points)
    table = np.zeros((len(where), count))
    for i, spot in enumerate(where):
        for j in range(count):
            total = 0.0
            for k in range(count):
                if k == j:
                    continue
                term = 1.0 / (points[j] - points[k])
                for m in range(count):
                    if m != j and m != k:
                        term = term * (spot - points[m]) / (points[j] - points[m])
                total = total + term
            table[i, j] = total
    return table


def tables():
    points, weights = gll_points()
    slopes = lagrange_slopes(points, points)
    eye = np.eye(5)
    forward = np.zeros((3, 128, 256))
    weight = np.zeros((128,))
    mass = np.zeros((PER,))
    interp = np.zeros((PER, 8))
    for d in range(3):
        tx, ty, tz = (slopes if d == a else eye for a in range(3))
        full = np.einsum("Jj,Kk,Ii->JKIjki", ty, tz, tx)
        wide = np.zeros((5, 5, 5, 5, 5, 8))
        wide[..., :5] = full
        forward[d, :125, :PER] = wide.reshape(125, PER)
    cube = weights[:, None, None] * weights[None, :, None] * weights[None, None, :]
    weight[:125] = cube.reshape(-1)
    mass_wide = np.zeros((5, 5, 8))
    mass_wide[..., :5] = MASS_COEF * cube
    mass[:] = mass_wide.reshape(-1)
    line = np.stack([1.0 - points, points], 1)
    line8 = np.zeros((8, 2))
    line8[:5] = line
    interp[:] = np.einsum("Jj,Kk,Ii->JKIjki", line, line, line8).reshape(PER, 8)
    gauss = np.array([0.5 - 0.5 / math.sqrt(3.0), 0.5 + 0.5 / math.sqrt(3.0)])
    basis = np.stack([1.0 - gauss, gauss], 1)
    steep = np.array([[-1.0, 1.0], [-1.0, 1.0]])
    coarse = np.zeros((32, 8))
    for d in range(4):
        tx, ty, tz = (steep if d == a else basis for a in range(3))
        coarse[d * 8 : d * 8 + 8] = np.einsum("Jj,Kk,Ii->JKIjki", ty, tz, tx).reshape(8, 8)
    flat = forward.reshape(384, 256)
    parts = (
        flat,
        flat[:, :PER].T,
        np.broadcast_to(weight[:, None], (128, LANES)),
        np.broadcast_to(mass[:, None], (PER, LANES)),
        interp,
        interp.T,
        coarse,
        coarse.T,
    )
    return [jnp.asarray(np.ascontiguousarray(part), dtype=jnp.float32) for part in parts]


def dot(a, b):
    return jnp.dot(a, b, precision=HIGHEST, preferred_element_type=jnp.float32)


def stresses(grad, fibre, scale):
    shear = {}
    for i in range(3):
        for j in range(i, 3):
            shear[i, j] = grad[i][i] if i == j else 0.5 * (grad[i][j] + grad[j][i])
            shear[j, i] = shear[i, j]
    trace = LAMBDA_COEF * (shear[0, 0] + shear[1, 1] + shear[2, 2])
    along = [
        shear[i, 0] * fibre[0] + shear[i, 1] * fibre[1] + shear[i, 2] * fibre[2] for i in range(3)
    ]
    stretch = fibre[0] * along[0] + fibre[1] * along[1] + fibre[2] * along[2]
    half = (0.5 * FIBRE_COEF) * stretch
    cross = 2.0 * (SHEAR_ALONG - SHEAR_CROSS)
    pull = [cross * along[i] + half * fibre[i] for i in range(3)]
    out = {}
    for i in range(3):
        for j in range(i, 3):
            value = 2.0 * SHEAR_CROSS * shear[i, j] + (fibre[i] * pull[j] + pull[i] * fibre[j])
            if i == j:
                value = value + trace
            out[i, j] = out[j, i] = value * scale
    return out


def estimate(n):
    scale = 1.0 / jnp.sqrt(n[0] + 1e-6)
    last = None
    for k in range(1, 4):
        last = jnp.sqrt((n[k] * scale) * scale + 1e-6)
        scale = scale / last
    return last


def smoothing(largest, ratio):
    upper = 1.1 * largest
    lower = upper / ratio
    centre = 0.5 * (upper + lower)
    radius = 0.5 * (upper - lower)
    spread = centre / radius
    weight = 1.0 / spread
    step = [1.0 / centre]
    rest = [jnp.ones_like(largest)]
    total = [jnp.zeros_like(largest)] * 4

    def entry(poly, n):
        return poly[n] if n < len(poly) else jnp.zeros_like(largest)

    for k in range(4):
        total = [total[n] + entry(step, n) for n in range(4)]
        rest = [entry(rest, n) - (step[n - 1] if n > 0 else 0.0) for n in range(k + 2)]
        if k < 3:
            new = 1.0 / (2.0 * spread - weight)
            step = [
                new * weight * entry(step, n) + 2.0 * new / radius * rest[n] for n in range(k + 2)
            ]
            weight = new
    return total, rest


def group_peers(stage, wide, cross):
    chip, row = lax.rem(wide, 8), wide // 8
    if stage == 0:
        return [(row * 8 + lax.rem(chip + k, 8), cross) for k in range(1, 8)]
    spot = row * 4 + cross
    out = []
    for k in range(1, 16):
        other = lax.rem(spot + k, 16)
        out.append((other // 4 * 8 + chip, lax.rem(other, 4)))
    return out


def kernel(
    start_ref, rhs_ref, elem_ref, fwd_ref, bwd_ref, weight_ref, mass_ref, interp_ref, interp_t_ref,
    cgrad_ref, cgrad_t_ref,
    out_ref, cor_ref,
    held, mass_w, grad, send_x, send_y, send_e, got_x, got_y, got_e, csend, cgot, sums, got_a, got_b,
    send_sem, recv_sem, csend_sem, crecv_sem, sum_send, sum_recv,
):
    wide, cross = lax.axis_index("wide"), lax.axis_index("cross")
    n_wide, n_cross = lax.axis_size("wide"), lax.axis_size("cross")

    def present(n):
        dx, dy = NEIGHBOURS[n]
        inside = None
        for here, by, size in ((wide, dx, n_wide), (cross, dy, n_cross)):
            if by:
                ok = here > 0 if by < 0 else here < size - 1
                inside = ok if inside is None else inside & ok
        return inside

    def place(n):
        dx, dy = NEIGHBOURS[n]
        return (wide + dx, cross + dy)

    def opposite(n):
        dx, dy = NEIGHBOURS[n]
        return NEIGHBOURS.index((-dx, -dy))

    got_x[...] = jnp.zeros_like(got_x)
    got_y[...] = jnp.zeros_like(got_y)
    got_e[...] = jnp.zeros_like(got_e)
    cgot[...] = jnp.zeros_like(cgot)
    barrier = pltpu.get_barrier_semaphore()
    expected = jnp.int32(0)
    for n in range(8):
        @pl.when(present(n))
        def _(n=n):
            pl.semaphore_signal(barrier, inc=1, device_id=place(n), device_id_type=MESH)
        expected = expected + present(n).astype(jnp.int32)
    for stage in range(2):
        for peer in group_peers(stage, wide, cross):
            pl.semaphore_signal(barrier, inc=1, device_id=peer, device_id_type=MESH)
            expected = expected + 1

    held[...] = jnp.zeros_like(held)
    send_x[...] = jnp.zeros_like(send_x)
    send_y[...] = jnp.zeros_like(send_y)
    send_e[...] = jnp.zeros_like(send_e)
    sums[...] = jnp.zeros_like(sums)
    mass_w[...] = weight_ref[...] * elem_ref[3:4, :]
    held[0, :ROWS] = start_ref[...]
    pl.semaphore_wait(barrier, expected)

    lane = lax.broadcasted_iota(jnp.int32, (8, LANES), 1)
    sub = lax.broadcasted_iota(jnp.int32, (8, LANES), 0)
    spot = lax.rem(lane, 64)
    low = lane < 64
    one_x = jnp.where(wide < n_wide - 1, 1.0, 0.0)
    one_y = jnp.where(cross < n_cross - 1, 1.0, 0.0)
    keep_y = jnp.where(low, 1.0, one_y)

    def spread_to(mask, rows):
        return jnp.broadcast_to(mask[:1], (rows, LANES))

    def sides(s, n):
        if n < 2:
            return send_x.at[s, n], got_x.at[s, n], got_x.at[s, opposite(n)]
        if n < 4:
            return send_y.at[s, n - 2], got_y.at[s, n - 2], got_y.at[s, opposite(n) - 2]
        return send_e.at[s, n - 4], got_e.at[s, n - 4], got_e.at[s, opposite(n) - 4]

    def outgoing(s, n):
        source, _, target = sides(s, n)
        return pltpu.make_async_remote_copy(
            src_ref=source, dst_ref=target, send_sem=send_sem.at[s, n],
            recv_sem=recv_sem.at[s, opposite(n)], device_id=place(n), device_id_type=MESH)

    def incoming(s, n):
        source, target, _ = sides(s, n)
        return pltpu.make_async_remote_copy(
            src_ref=source, dst_ref=target, send_sem=send_sem.at[s, n],
            recv_sem=recv_sem.at[s, n], device_id=place(n), device_id_type=MESH)

    def exchange(t, s):
        for side in range(2):
            send_x[s, side, :75] = held[t, pl.ds(4 * side, 75, stride=8)]
            face = jnp.concatenate(
                [held[t, c * PER + side * 160 : c * PER + side * 160 + 40] for c in range(3)], 0)
            first, second = face[:64], face[64:]
            rolled = pltpu.roll(second, 64, 1)
            use = spread_to(low if side == 0 else ~low, 56)
            send_y[s, side, :56] = jnp.where(use, first[:56], rolled)
            send_y[s, side, 56:] = first[56:]
        for n in range(4, 8):
            dx, dy = NEIGHBOURS[n]
            i, j = (4 if dx > 0 else 0), (4 if dy > 0 else 0)
            for c in range(3):
                send_e[s, n - 4, c * 8 : c * 8 + 5] = held[
                    t, pl.ds(c * PER + j * 40 + i, 5, stride=8)]
        for n in (4, 5, 6, 7, 0, 1, 2, 3):
            @pl.when(present(n))
            def _(n=n):
                outgoing(s, n).start()
        for n in range(8):
            @pl.when(present(n))
            def _(n=n):
                incoming(s, n).wait_recv()
        for side in range(2):
            got = got_y[s, side]
            use = spread_to(low if side == 0 else ~low, 64)
            first = jnp.where(use, pltpu.roll(got, 64, 1), 0.0)
            second = jnp.where(use[:56], got[:56], 0.0)
            more = jnp.concatenate([first, second], 0)
            for c in range(3):
                at = c * PER + side * 160
                value = held[t, at : at + 40] + more[c * 40 : c * 40 + 40]
                held[t, at : at + 40] = value
        for side in range(2):
            value = held[t, pl.ds(4 * side, 75, stride=8)] + got_x[s, side, :75]
            held[t, pl.ds(4 * side, 75, stride=8)] = value
        for n in range(4, 8):
            dx, dy = NEIGHBOURS[n]
            i, j = (4 if dx > 0 else 0), (4 if dy > 0 else 0)
            use = low if dy < 0 else ~low
            for c in range(3):
                more = jnp.where(use, pltpu.roll(got_e[s, n - 4, c * 8 : c * 8 + 8], 64, 1), 0.0)
                at = pl.ds(c * PER + j * 40 + i, 5, stride=8)
                held[t, at] = held[t, at] + more[:5]
        held[t, pl.ds(4, 75, stride=8)] = held[t, pl.ds(4, 75, stride=8)] * one_x
        for c in range(3):
            at = c * PER + 160
            held[t, at : at + 40] = held[t, at : at + 40] * spread_to(keep_y, 40)
        for n in range(8):
            @pl.when(present(n))
            def _(n=n):
                outgoing(s, n).wait_send()

    fibre = [elem_ref[i : i + 1, :] for i in range(3)]

    def elements(t):
        block = jnp.concatenate([held[t, c * PER : c * PER + 256] for c in range(3)], 1)
        grad[...] = dot(fwd_ref[...], block)

        def tile(q, carry):
            at = pl.multiple_of(q * 16, 16)
            g = [[grad[pl.ds(d * 128 + at, 16), c * 128 : c * 128 + 128] for d in range(3)]
                 for c in range(3)]
            part = stresses(g, fibre, mass_w[pl.ds(at, 16), :])
            for c in range(3):
                for d in range(3):
                    grad[pl.ds(d * 128 + at, 16), c * 128 : c * 128 + 128] = part[c, d]
            return carry

        lax.fori_loop(0, 8, tile, 0, unroll=True)
        result = dot(bwd_ref[...], grad[...])
        return [
            result[:, c * 128 : c * 128 + 128] + mass_ref[...] * held[t, c * PER : c * PER + PER]
            for c in range(3)
        ]

    inner = spread_to(spot > 0, 8)
    outer = spread_to(spot < 63, 8)

    def gather_local(t):
        for c in range(3):
            for j in range(5):
                at = c * PER + j * 40
                first, last = held[t, at : at + 8], held[t, at + 32 : at + 40]
                held[t, at : at + 8] = first + jnp.where(inner, pltpu.roll(last, 1, 1), 0.0)
                held[t, at + 32 : at + 40] = last + jnp.where(outer, pltpu.roll(first, 127, 1), 0.0)
            at = c * PER
            first, last = held[t, at : at + 40], held[t, at + 160 : at + 200]
            use = spread_to(low, 40)
            held[t, at : at + 40] = first + jnp.where(use, 0.0, pltpu.roll(last, 64, 1))
            held[t, at + 160 : at + 200] = last + jnp.where(use, pltpu.roll(first, 64, 1), 0.0)

    ends = spread_to(spot == 63, 8)

    def square(t):
        total = jnp.zeros((8, LANES), jnp.float32)
        tail = jnp.zeros((8, LANES), jnp.float32)
        for c in range(3):
            for j in range(4):
                for k in range(5):
                    at = c * PER + j * 40 + k * 8
                    v = held[t, at : at + 8]
                    if k < 4:
                        total = total + v * v
                    else:
                        tail = tail + v * v
        total = total + jnp.where(ends, tail, 0.0)
        total = jnp.where(sub < 4, total, 0.0)
        return jnp.sum(total, axis=0, keepdims=True)

    def all_sum(slot):
        for stage in range(2):
            got = (got_a, got_b)[stage]
            copies = [
                pltpu.make_async_remote_copy(
                    src_ref=sums.at[slot, stage], dst_ref=got.at[slot, k],
                    send_sem=sum_send.at[slot, stage, k], recv_sem=sum_recv.at[slot, stage, k],
                    device_id=peer, device_id_type=MESH)
                for k, peer in enumerate(group_peers(stage, wide, cross))
            ]
            for copy in copies:
                copy.start()
            for copy in copies:
                copy.wait_recv()
            total = sums[slot, stage]
            for k in range(len(copies)):
                total = total + got[slot, k]
            for copy in copies:
                copy.wait_send()
            if stage == 0:
                sums[slot, 1] = total
        return jnp.sum(total, axis=1, keepdims=True)

    def four_steps(base):
        def step(t, carry):
            parts = elements(t)
            for c in range(3):
                at = c * PER
                held[t + 1, at : at + PER] = parts[c]
            gather_local(t + 1)

            @pl.when(t == 0)
            def _():
                held[1, :ROWS] = rhs_ref[...] - held[1, :ROWS]

            exchange(t + 1, lax.rem(t + base, 2))
            return carry

        lax.fori_loop(0, 4, step, 0)

    exchange(0, 0)
    four_steps(1)
    for n in range(4):
        sums[0, 0, n : n + 1] = square(n + 1)
    norms = all_sum(0)
    largest = jnp.broadcast_to(estimate([norms[n : n + 1] for n in range(4)]), (1, LANES))
    step_poly, rest_poly = smoothing(largest, FINE_RATIO)

    parts = elements(4)
    row = lax.broadcasted_iota(jnp.int32, (PER, LANES), 0)
    wide_lane = lax.broadcasted_iota(jnp.int32, (PER, LANES), 1)
    at_i, at_k, at_j = lax.rem(row, 8), lax.rem(row // 8, 5), row // 40
    owned = (at_i < 4) & (at_j < 4) & ((at_k < 4) | (lax.rem(wide_lane, 64) == 63))
    free = ((at_i < 4) | (wide < n_wide - 1)) & (
        (at_j < 4) | (wide_lane < 64) | (cross < n_cross - 1))
    for c in range(3):
        at = c * PER
        kept = [held[n + 1, at : at + PER] for n in range(4)]
        value = rest_poly[0] * kept[0]
        more = step_poly[0] * kept[0]
        for n in range(1, 4):
            value = value + rest_poly[n] * kept[n]
            more = more + step_poly[n] * kept[n]
        value = jnp.where(owned, value, 0.0) + jnp.where(free, rest_poly[4] * parts[c], 0.0)
        held[0, at : at + PER] = held[0, at : at + PER] + more
        csend[0, c * 8 : c * 8 + 8] = dot(interp_t_ref[...], value)

    bit_i, bit_k, bit_j = lax.rem(sub, 2) == 1, lax.rem(sub // 2, 2) == 1, sub >= 4
    drop = (bit_i & (wide == n_wide - 1)) | (bit_j & ~low & (cross == n_cross - 1))
    cfree = jnp.where(drop, 0.0, 1.0)

    def swap(v, by, bit):
        return jnp.where(bit, pltpu.roll(v, by, 0), pltpu.roll(v, 8 - by, 0))

    def coarse_copy(s, n, m):
        return pltpu.make_async_remote_copy(
            src_ref=csend.at[s], dst_ref=cgot.at[s, m], send_sem=csend_sem.at[s, n],
            recv_sem=crecv_sem.at[s, m], device_id=place(n), device_id_type=MESH)

    def coarse_exchange(s):
        for c in range(3):
            v = csend[s, c * 8 : c * 8 + 8]
            other = swap(v, 2, bit_k)
            v = v + jnp.where(
                bit_k, jnp.where(spot < 63, pltpu.roll(other, 127, 1), 0.0),
                jnp.where(spot > 0, pltpu.roll(other, 1, 1), 0.0))
            other = pltpu.roll(swap(v, 4, bit_j), 64, 1)
            v = v + jnp.where(bit_j == low, other, 0.0)
            csend[s, c * 8 : c * 8 + 8] = v
        for n in (4, 5, 6, 7, 0, 1, 2, 3):
            @pl.when(present(n))
            def _(n=n):
                coarse_copy(s, n, opposite(n)).start()
        for n in range(8):
            @pl.when(present(n))
            def _(n=n):
                coarse_copy(s, n, n).wait_recv()
        out = []
        for c in range(3):
            v = csend[s, c * 8 : c * 8 + 8]
            for n in range(8):
                dx, dy = NEIGHBOURS[n]
                got = cgot[s, n, c * 8 : c * 8 + 8]
                use = None
                if dx:
                    got = swap(got, 1, bit_i)
                    use = bit_i if dx > 0 else ~bit_i
                if dy:
                    got = pltpu.roll(swap(got, 4, bit_j), 64, 1)
                    side = (bit_j & ~low) if dy > 0 else (~bit_j & low)
                    use = side if use is None else use & side
                v = v + jnp.where(use, got, 0.0)
            out.append(v * cfree)
        for n in range(8):
            @pl.when(present(n))
            def _(n=n):
                coarse_copy(s, n, opposite(n)).wait_send()
        return out

    coarse_scale = 0.125 * elem_ref[3:4, :]

    def coarse_elements(vec, s):
        block = jnp.concatenate(vec, 1)
        g = dot(cgrad_ref[...], block)
        part = stresses(
            [[g[d * 8 : d * 8 + 8, c * 128 : c * 128 + 128] for d in range(3)] for c in range(3)],
            fibre, coarse_scale)
        for c in range(3):
            stack = jnp.concatenate(
                [part[c, d] for d in range(3)]
                + [(0.125 * MASS_COEF) * g[24:32, c * 128 : c * 128 + 128]], 0)
            csend[s, c * 8 : c * 8 + 8] = dot(cgrad_t_ref[...], stack)

    own_c = ~bit_i & ~bit_j & (~bit_k | (spot == 63))

    def coarse_square(vec):
        total = vec[0] * vec[0] + vec[1] * vec[1] + vec[2] * vec[2]
        return jnp.sum(jnp.where(own_c, total, 0.0), axis=0, keepdims=True)

    vectors = [coarse_exchange(0)]
    sums[1, 0, 0:1] = coarse_square(vectors[0])
    for n in range(1, 4):
        coarse_elements(vectors[-1], n % 2)
        vectors.append(coarse_exchange(n % 2))
        sums[1, 0, n : n + 1] = coarse_square(vectors[-1])
    norms = all_sum(1)
    coarse_largest = jnp.broadcast_to(estimate([norms[n : n + 1] for n in range(4)]), (1, LANES))
    coarse_poly, _ = smoothing(coarse_largest, COARSE_RATIO)
    for c in range(3):
        value = coarse_poly[0] * vectors[0][c]
        for n in range(1, 4):
            value = value + coarse_poly[n] * vectors[n][c]
        cor_ref[c * 8 : c * 8 + 8] = value
        at = c * PER
        held[0, at : at + PER] = held[0, at : at + PER] + dot(interp_ref[...], value)

    four_steps(1)
    for c in range(3):
        at = c * PER
        value = held[0, at : at + PER]
        for n in range(4):
            value = value + step_poly[n] * held[n + 1, at : at + PER]
        out_ref[at : at + PER] = value


def to_rows(field):
    z = jnp.concatenate(
        [field[..., :-1].reshape(3, 4, 8, 64, 4), field[..., 4::4][..., None]], -1)
    z = jnp.pad(z, ((0, 0), (0, 4), (0, 1), (0, 0), (0, 0)))
    y = jnp.stack([z[:, :, :5], z[:, :, 4:]], 2)
    return jnp.transpose(y, (0, 3, 5, 1, 2, 4)).reshape(ROWS, LANES)


def from_rows(rows):
    view = rows.reshape(3, 5, 5, 8, 2, 64)[:, :4, :, :4]
    view = jnp.transpose(view, (0, 3, 4, 1, 5, 2)).reshape(3, 4, 8, 64, 5)
    return jnp.concatenate(
        [view[..., :4].reshape(3, 4, 8, 256), view[:, :, :, -1:, 4]], -1)


def fibre_vectors(index):
    angle = index.astype(jnp.float32) * (2.0 * math.pi / NFIB)
    tilt = 0.4 * jnp.sin(3.0 * angle)
    return jnp.stack(
        [jnp.cos(angle) * jnp.cos(tilt), jnp.sin(angle) * jnp.cos(tilt), jnp.sin(tilt)]
    )


def on_device(rhs, start, stiffness, fibre_index):
    fibre = fibre_vectors(fibre_index).reshape(3, LANES)
    elem = jnp.concatenate([fibre, stiffness.reshape(1, LANES), jnp.zeros((4, LANES))], 0)
    operands = [to_rows(start), to_rows(rhs), elem] + tables()
    vmem = pl.BlockSpec(memory_space=pltpu.VMEM)
    f32 = jnp.float32
    rows, coarse = pl.pallas_call(
        kernel,
        out_shape=(
            jax.ShapeDtypeStruct((ROWS, LANES), f32),
            jax.ShapeDtypeStruct((24, LANES), f32),
        ),
        in_specs=[vmem] * len(operands),
        out_specs=(vmem, vmem),
        scratch_shapes=[
            pltpu.VMEM((5, HELD, LANES), f32),
            pltpu.VMEM((128, LANES), f32),
            pltpu.VMEM((384, 384), f32),
            pltpu.VMEM((2, 2, FACE_X, LANES), f32),
            pltpu.VMEM((2, 2, FACE_Y, LANES), f32),
            pltpu.VMEM((2, 4, EDGE, LANES), f32),
            pltpu.VMEM((2, 2, FACE_X, LANES), f32),
            pltpu.VMEM((2, 2, FACE_Y, LANES), f32),
            pltpu.VMEM((2, 4, EDGE, LANES), f32),
            pltpu.VMEM((2, 24, LANES), f32),
            pltpu.VMEM((2, 8, 24, LANES), f32),
            pltpu.VMEM((2, 2, 8, LANES), f32),
            pltpu.VMEM((2, 7, 8, LANES), f32),
            pltpu.VMEM((2, 15, 8, LANES), f32),
            pltpu.SemaphoreType.DMA((2, 8)),
            pltpu.SemaphoreType.DMA((2, 8)),
            pltpu.SemaphoreType.DMA((2, 8)),
            pltpu.SemaphoreType.DMA((2, 8)),
            pltpu.SemaphoreType.DMA((2, 2, 15)),
            pltpu.SemaphoreType.DMA((2, 2, 15)),
        ],
        compiler_params=pltpu.CompilerParams(
            collective_id=0, has_side_effects=True, vmem_limit_bytes=32 * 1024 * 1024
        ),
    )(*operands)
    view = coarse.reshape(3, 2, 2, 2, 2, 64)[:, 0, :, 0]
    correction = jnp.concatenate([view[:, 0], view[:, 1, :, -1:]], -1)[:, None]
    return from_rows(rows), correction


def solution(mesh):
    in_specs = (
        P(None, "wide", "cross", None),
        P(None, "wide", "cross", None),
        P("wide", "cross", None),
        P("wide", "cross", None),
    )
    out_specs = (P(None, "wide", "cross", None), P(None, "wide", "cross", None))
    return jax.shard_map(
        on_device, mesh=mesh, in_specs=in_specs, out_specs=out_specs, check_vma=False
    )
```

```python
import functools
import math

import jax
import jax.numpy as jnp
import numpy as np
from jax import lax
from jax.experimental import pallas as pl
from jax.experimental.pallas import tpu as pltpu
from jax.sharding import PartitionSpec as P

NFIB = 64
LAMBDA_COEF = 2.0
SHEAR_CROSS = 1.0
SHEAR_ALONG = 3.0
FIBRE_COEF = 20.0
MASS_COEF = 0.02
FINE_RATIO = 10.0
COARSE_RATIO = 30.0

MESH = pl.DeviceIdType.MESH
LANES = 128
PER = 200
ROWS = 3 * PER
NEIGHBOURS = ((-1, 0), (1, 0), (0, -1), (0, 1), (-1, -1), (-1, 1), (1, -1), (1, 1))
FACE_X, FACE_Y, EDGE = 80, 64, 24
REACH = (-4, -3, -2, -1, 1, 2, 3, 4)
HOME = 3


def gll_points():
    root = math.sqrt(3.0 / 7.0)
    points = (np.array([-1.0, -root, 0.0, root, 1.0]) + 1.0) / 2.0
    weights = np.array([0.1, 49.0 / 90.0, 32.0 / 45.0, 49.0 / 90.0, 0.1]) / 2.0
    return (points, weights)


def lagrange_slopes(points, where):
    count = len(points)
    table = np.zeros((len(where), count))
    for i, spot in enumerate(where):
        for j in range(count):
            total = 0.0
            for k in range(count):
                if k == j:
                    continue
                term = 1.0 / (points[j] - points[k])
                for m in range(count):
                    if m != j and m != k:
                        term = term * (spot - points[m]) / (points[j] - points[m])
                total = total + term
            table[i, j] = total
    return table


def tables():
    points, weights = gll_points()
    slopes = lagrange_slopes(points, points)
    cube = np.zeros((5, 5, 8))
    cube[..., :5] = weights[:, None, None] * weights[None, :, None] * weights[None, None, :]
    columns = np.zeros((12, 8, LANES))
    columns[0:5, :5] = slopes.T[:, :, None]
    columns[5:10, :5] = slopes[:, :, None]
    columns[10, :5] = (1.0 - points)[:, None]
    columns[11, :5] = points[:, None]
    parts = (
        np.broadcast_to(cube.reshape(-1)[:, None], (PER, LANES)),
        columns.reshape(96, LANES),
    )
    return [jnp.asarray(np.ascontiguousarray(part), dtype=jnp.float32) for part in parts]


def dot(a, b):
    return jnp.dot(
        a, b, precision=lax.Precision.HIGHEST, preferred_element_type=jnp.float32
    )


GAUSS = 0.5 / math.sqrt(3.0)


def to_gauss(u0, u1):
    slope = u1 - u0
    middle = u0 + 0.5 * slope
    part = GAUSS * slope
    return middle - part, middle + part, slope


def from_gauss(a0, a1, slope=None):
    both = a0 + a1
    last = 0.5 * both + GAUSS * (a1 - a0)
    if slope is not None:
        last = last + slope
    return both - last, last


def along_line(u, table):
    half = lambda i, j: 0.5 * (float(table[i, j]) + float(table[i, 4 - j]))
    odd_half = lambda i, j: 0.5 * (float(table[i, j]) - float(table[i, 4 - j]))
    even = [u[0] + u[4], u[1] + u[3]]
    odd = [u[0] - u[4], u[1] - u[3]]
    p = [
        half(i, 0) * even[0] + half(i, 1) * even[1] + float(table[i, 2]) * u[2] for i in range(2)
    ]
    q = [odd_half(i, 0) * odd[0] + odd_half(i, 1) * odd[1] for i in range(3)]
    return [q[0] + p[0], q[1] + p[1], q[2], q[1] - p[1], q[0] - p[0]]


def stresses(grad, fibre, scale):
    shear = {}
    for i in range(3):
        for j in range(i, 3):
            shear[i, j] = grad[i][i] if i == j else 0.5 * (grad[i][j] + grad[j][i])
            shear[j, i] = shear[i, j]
    trace = LAMBDA_COEF * (shear[0, 0] + shear[1, 1] + shear[2, 2])
    along = [
        shear[i, 0] * fibre[0] + shear[i, 1] * fibre[1] + shear[i, 2] * fibre[2] for i in range(3)
    ]
    stretch = fibre[0] * along[0] + fibre[1] * along[1] + fibre[2] * along[2]
    half = (0.5 * FIBRE_COEF) * stretch
    cross = 2.0 * (SHEAR_ALONG - SHEAR_CROSS)
    pull = [cross * along[i] + half * fibre[i] for i in range(3)]
    out = {}
    for i in range(3):
        for j in range(i, 3):
            value = 2.0 * SHEAR_CROSS * shear[i, j] + (fibre[i] * pull[j] + pull[i] * fibre[j])
            if i == j:
                value = value + trace
            out[i, j] = out[j, i] = value * scale
    return out


def estimate(n):
    scale = 1.0 / jnp.sqrt(n[0] + 1e-6)
    last = None
    for k in range(1, 4):
        last = jnp.sqrt((n[k] * scale) * scale + 1e-6)
        scale = scale / last
    return last


def smoothing(largest, ratio):
    upper = 1.1 * largest
    lower = upper / ratio
    centre = 0.5 * (upper + lower)
    radius = 0.5 * (upper - lower)
    spread = centre / radius
    weight = 1.0 / spread
    step = [1.0 / centre]
    rest = [jnp.ones_like(largest)]
    total = [jnp.zeros_like(largest)] * 4

    def entry(poly, n):
        return poly[n] if n < len(poly) else jnp.zeros_like(largest)

    for k in range(4):
        total = [total[n] + entry(step, n) for n in range(4)]
        rest = [entry(rest, n) - (step[n - 1] if n > 0 else 0.0) for n in range(k + 2)]
        if k < 3:
            new = 1.0 / (2.0 * spread - weight)
            step = [
                new * weight * entry(step, n) + 2.0 * new / radius * rest[n] for n in range(k + 2)
            ]
            weight = new
    return total, rest


def kernel(
    start_ref, rhs_ref, elem_ref, weight_ref, column_ref,
    out_ref, cor_ref,
    held, load, mass_w, slope_y, flux_x, flux_y, planes,
    send_x, send_y, send_e, got_x, got_y, got_e,
    rest, coarse_out, reach_in, elem_z, elem_out, elem_in, elem_c, vertex, gather,
    sums, got_z, got_w,
    send_sem, recv_sem, z_send, z_recv, w_send, w_recv, ez_send, ez_recv, cz_send, cz_recv,
    er_send, er_recv, cr_send, cr_recv,
):
    wide, cross = lax.axis_index("wide"), lax.axis_index("cross")
    n_wide, n_cross = lax.axis_size("wide"), lax.axis_size("cross")
    f32 = jnp.float32

    def within(at, by, size):
        return at >= -by if by < 0 else at < size - by

    def present(n):
        dx, dy = NEIGHBOURS[n]
        inside = None
        for here, by, size in ((wide, dx, n_wide), (cross, dy, n_cross)):
            if by:
                ok = within(here, by, size)
                inside = ok if inside is None else inside & ok
        return inside

    def place(n):
        dx, dy = NEIGHBOURS[n]
        return (wide + dx, cross + dy)

    def opposite(n):
        dx, dy = NEIGHBOURS[n]
        return NEIGHBOURS.index((-dx, -dy))

    z_peers = [(wide, lax.rem(cross + k, n_cross)) for k in range(1, n_cross)]
    w_peers = [(lax.rem(wide + k, n_wide), cross) for k in range(1, n_wide)]

    got_x[...] = jnp.zeros_like(got_x)
    got_y[...] = jnp.zeros_like(got_y)
    got_e[...] = jnp.zeros_like(got_e)
    reach_in[...] = jnp.zeros_like(reach_in)
    elem_in[...] = jnp.zeros_like(elem_in)
    barrier = pltpu.get_barrier_semaphore()
    expected = jnp.int32(len(z_peers) + len(w_peers))
    for peer in z_peers + w_peers:
        pl.semaphore_signal(barrier, inc=1, device_id=peer, device_id_type=MESH)
    for n in range(4, 8):
        @pl.when(present(n))
        def _(n=n):
            pl.semaphore_signal(barrier, inc=1, device_id=place(n), device_id_type=MESH)
        expected = expected + present(n).astype(jnp.int32)

    lane = lax.broadcasted_iota(jnp.int32, (8, LANES), 1)
    sub = lax.broadcasted_iota(jnp.int32, (8, LANES), 0)
    spot = lax.rem(lane, 64)
    low = lane < 64
    ends = spot == 63
    one_x = jnp.where(wide < n_wide - 1, 1.0, 0.0)
    one_y = jnp.where(cross < n_cross - 1, 1.0, 0.0)
    keep_y = jnp.where(low, 1.0, one_y)

    def spread_to(mask, rows):
        return jnp.broadcast_to(mask[:1], (rows, LANES))

    send_x[...] = jnp.zeros_like(send_x)
    send_e[...] = jnp.zeros_like(send_e)
    sums[...] = jnp.zeros_like(sums)
    vertex[...] = jnp.zeros_like(vertex)
    gather[...] = jnp.zeros_like(gather)
    mass_w[...] = weight_ref[...] * elem_ref[3:4, :]
    elem_z[cross] = elem_ref[...]

    z_at = lax.broadcasted_iota(jnp.int32, (256, 5 * LANES), 0)
    col = lax.broadcasted_iota(jnp.int32, (256, 5 * LANES), 1)
    pick = jnp.where(z_at == 4 * lax.rem(col, 64) + col // LANES, 1.0, 0.0)

    def unpack(ref, into):
        nodes = dot(ref[:, :, :, 0:256].reshape(96, 256), pick)
        final = jnp.broadcast_to(ref[:, :, :, 256:257].reshape(96, 1), (96, LANES))
        for k in range(5):
            part = nodes[:, k * LANES : k * LANES + LANES]
            planes[k] = jnp.where(spread_to(ends, 96), final, part) if k == 4 else part
        into[...] = jnp.zeros_like(into)
        for c in range(3):
            for j in range(5):
                for k in range(5):
                    first = planes[k, pl.ds(c * 32 + j, 4, stride=8)]
                    if j < 4:
                        second = planes[k, pl.ds(c * 32 + 4 + j, 4, stride=8)]
                    else:
                        second = jnp.zeros((4, LANES), f32)
                    at = c * PER + j * 40 + k * 8
                    into[at : at + 4] = jnp.where(low[:4], first, second)

    unpack(start_ref, held.at[0])
    pl.semaphore_wait(barrier, expected)

    def z_copy(source, target, sem_out, sem_in, k, back=False):
        return pltpu.make_async_remote_copy(
            src_ref=source, dst_ref=target, send_sem=sem_out.at[k - 1], recv_sem=sem_in.at[k - 1],
            device_id=z_peers[k - 1], device_id_type=MESH)

    def from_z(k):
        return lax.rem(cross + n_cross - k, n_cross)

    def reach_out(source, into, sem_out, sem_in, m):
        back = REACH.index(-REACH[m])
        return pltpu.make_async_remote_copy(
            src_ref=source, dst_ref=into.at[back], send_sem=sem_out.at[m], recv_sem=sem_in.at[back],
            device_id=(wide + REACH[m], cross), device_id_type=MESH)

    def reach_back(source, into, sem_out, sem_in, m):
        return pltpu.make_async_remote_copy(
            src_ref=source, dst_ref=into.at[m], send_sem=sem_out.at[m], recv_sem=sem_in.at[m],
            device_id=(wide + REACH[m], cross), device_id_type=MESH)

    def each_reach(make, act):
        for m, by in enumerate(REACH):
            @pl.when(within(wide, by, n_wide))
            def _(m=m):
                act(make(m))

    def sides(s, n):
        if n < 2:
            return send_x.at[s, n], got_x.at[s, n], got_x.at[s, opposite(n)]
        if n < 4:
            return send_y.at[s, n - 2], got_y.at[s, n - 2], got_y.at[s, opposite(n) - 2]
        return send_e.at[s, n - 4], got_e.at[s, n - 4], got_e.at[s, opposite(n) - 4]

    def outgoing(s, n):
        source, _, target = sides(s, n)
        return pltpu.make_async_remote_copy(
            src_ref=source, dst_ref=target, send_sem=send_sem.at[s, n],
            recv_sem=recv_sem.at[s, opposite(n)], device_id=place(n), device_id_type=MESH)

    def incoming(s, n):
        source, target, _ = sides(s, n)
        return pltpu.make_async_remote_copy(
            src_ref=source, dst_ref=target, send_sem=send_sem.at[s, n],
            recv_sem=recv_sem.at[s, n], device_id=place(n), device_id_type=MESH)

    def exchange_start(t, s):
        for n in range(4, 8):
            dx, dy = NEIGHBOURS[n]
            i, j = (4 if dx > 0 else 0), (4 if dy > 0 else 0)
            for c in range(3):
                send_e[s, n - 4, c * 8 : c * 8 + 5] = held[
                    t, pl.ds(c * PER + j * 40 + i, 5, stride=8)]
        for n in (4, 5, 6, 7):
            @pl.when(present(n))
            def _(n=n):
                outgoing(s, n).start()
        for side in range(2):
            send_x[s, side, :75] = held[t, pl.ds(4 * side, 75, stride=8)]
        for n in (0, 1):
            @pl.when(present(n))
            def _(n=n):
                outgoing(s, n).start()
        for side in range(2):
            face = jnp.concatenate(
                [held[t, c * PER + side * 160 : c * PER + side * 160 + 40] for c in range(3)], 0)
            first, second = face[:64], face[64:]
            rolled = pltpu.roll(second, 64, 1)
            use = spread_to(low if side == 0 else ~low, 56)
            send_y[s, side, :56] = jnp.where(use, first[:56], rolled)
            send_y[s, side, 56:] = first[56:]
        for n in (2, 3):
            @pl.when(present(n))
            def _(n=n):
                outgoing(s, n).start()

    def exchange_finish(t, s):
        for n in (2, 3):
            @pl.when(present(n))
            def _(n=n):
                incoming(s, n).wait_recv()
        for side in range(2):
            got = got_y[s, side]
            use = spread_to(low if side == 0 else ~low, 64)
            first = jnp.where(use, pltpu.roll(got, 64, 1), 0.0)
            second = jnp.where(use[:56], got[:56], 0.0)
            more = jnp.concatenate([first, second], 0)
            for c in range(3):
                at = c * PER + side * 160
                held[t, at : at + 40] = held[t, at : at + 40] + more[c * 40 : c * 40 + 40]
        for n in (0, 1):
            @pl.when(present(n))
            def _(n=n):
                incoming(s, n).wait_recv()
        for side in range(2):
            value = held[t, pl.ds(4 * side, 75, stride=8)] + got_x[s, side, :75]
            held[t, pl.ds(4 * side, 75, stride=8)] = value
        for n in (4, 5, 6, 7):
            @pl.when(present(n))
            def _(n=n):
                incoming(s, n).wait_recv()
        for n in range(4, 8):
            dx, dy = NEIGHBOURS[n]
            i, j = (4 if dx > 0 else 0), (4 if dy > 0 else 0)
            use = low if dy < 0 else ~low
            for c in range(3):
                more = jnp.where(use, pltpu.roll(got_e[s, n - 4, c * 8 : c * 8 + 8], 64, 1), 0.0)
                at = pl.ds(c * PER + j * 40 + i, 5, stride=8)
                held[t, at] = held[t, at] + more[:5]
        for n in range(8):
            @pl.when(present(n))
            def _(n=n):
                outgoing(s, n).wait_send()

    fibre = [elem_ref[i : i + 1, :] for i in range(3)]
    slopes = lagrange_slopes(gll_points()[0], gll_points()[0])

    def across(ref, at, table):
        total = None
        for i in range(5):
            row = jnp.broadcast_to(ref[pl.ds(at + i, 1), :], (8, LANES))
            term = column_ref[(table * 5 + i) * 8 : (table * 5 + i) * 8 + 8] * row
            total = term if total is None else total + term
        return total

    def elements(t, into):
        source = held.at[t]
        target = held.at[into]
        for c in range(3):
            for k in range(5):
                at = [c * PER + j * 40 + k * 8 for j in range(5)]
                for j, v in enumerate(along_line([source[a : a + 8] for a in at], slopes)):
                    slope_y[at[j] : at[j] + 8] = v

        def layer(j, carry):
            base = pl.multiple_of(j * 40, 8)

            def at(c, k):
                return pl.ds(pl.multiple_of(base + (c * PER + k * 8), 8), 8)

            grad_z = [along_line([source[at(c, k), :] for k in range(5)], slopes) for c in range(3)]
            flux_z = [[None] * 5 for _ in range(3)]
            for k in range(5):
                g = [
                    [across(source, base + (c * PER + k * 8), 0), slope_y[at(c, k), :], grad_z[c][k]]
                    for c in range(3)
                ]
                part = stresses(g, fibre, mass_w[at(0, k), :])
                for c in range(3):
                    flux_x[at(c, k), :] = part[c, 0]
                    flux_y[at(c, k), :] = part[c, 1]
                    flux_z[c][k] = part[c, 2]
            for c in range(3):
                pull = along_line(flux_z[c], slopes.T)
                for k in range(5):
                    mass = MASS_COEF * weight_ref[at(0, k), :] * source[at(c, k), :]
                    target[at(c, k), :] = (
                        pull[k] + mass + across(flux_x, base + (c * PER + k * 8), 1))
            return carry

        lax.fori_loop(0, 5, layer, 0)
        for c in range(3):
            for k in range(5):
                at = [c * PER + j * 40 + k * 8 for j in range(5)]
                for j, v in enumerate(along_line([flux_y[a : a + 8] for a in at], slopes.T)):
                    target[at[j] : at[j] + 8] = target[at[j] : at[j] + 8] + v

    inner = spread_to(spot > 0, 8)
    outer = spread_to(spot < 63, 8)

    def gather_local(t):
        for c in range(3):
            for j in range(5):
                at = c * PER + j * 40
                first, last = held[t, at : at + 8], held[t, at + 32 : at + 40]
                held[t, at : at + 8] = first + jnp.where(inner, pltpu.roll(last, 1, 1), 0.0)
                held[t, at + 32 : at + 40] = last + jnp.where(outer, pltpu.roll(first, 127, 1), 0.0)
            at = c * PER
            first, last = held[t, at : at + 40], held[t, at + 160 : at + 200]
            use = spread_to(low, 40)
            held[t, at : at + 40] = first + jnp.where(use, 0.0, pltpu.roll(last, 64, 1))
            held[t, at + 160 : at + 200] = spread_to(keep_y, 40) * (
                last + jnp.where(use, pltpu.roll(first, 64, 1), 0.0))
        held[t, pl.ds(4, 75, stride=8)] = held[t, pl.ds(4, 75, stride=8)] * one_x

    def square(t):
        total = jnp.zeros((8, LANES), f32)
        tail = jnp.zeros((8, LANES), f32)
        for c in range(3):
            for j in range(4):
                for k in range(5):
                    at = c * PER + j * 40 + k * 8
                    v = held[t, at : at + 8]
                    if k < 4:
                        total = total + v * v
                    else:
                        tail = tail + v * v
        total = total + jnp.where(ends, tail, 0.0)
        total = jnp.where(sub < 4, total, 0.0)
        return jnp.sum(total, axis=0, keepdims=True)

    def z_sums():
        return [
            z_copy(sums.at[0], got_z.at[k - 1], z_send, z_recv, k) for k in range(1, n_cross)
        ]

    def w_sums(slot):
        return [
            pltpu.make_async_remote_copy(
                src_ref=sums.at[slot], dst_ref=got_w.at[slot - 1, k],
                send_sem=w_send.at[slot - 1, k], recv_sem=w_recv.at[slot - 1, k],
                device_id=peer, device_id_type=MESH)
            for k, peer in enumerate(w_peers)
        ]

    def finish_sums(copies, own, got):
        for copy in copies:
            copy.wait_recv()
        total = own
        for k in range(len(copies)):
            total = total + got[k]
        for copy in copies:
            copy.wait_send()
        return total

    def apply_all(base):
        def step(t, carry):
            elements(t, t + 1)
            gather_local(t + 1)

            @pl.when(t == 0)
            def _():
                held[1] = load[...] - held[1]

            s = lax.rem(t + base, 2)
            exchange_start(t + 1, s)
            exchange_finish(t + 1, s)
            return carry

        lax.fori_loop(0, 4, step, 0)

    exchange_start(0, 0)
    for k in range(1, n_cross):
        z_copy(elem_z.at[cross], elem_z.at[cross], ez_send, ez_recv, k).start()
    unpack(rhs_ref, load)
    exchange_finish(0, 0)
    for k in range(1, n_cross):
        z_copy(elem_z.at[from_z(k)], elem_z.at[from_z(k)], ez_send, ez_recv, k).wait_recv()
    for q in range(4):
        for m in range(4):
            elem_out[m * 4 + q : m * 4 + q + 1] = elem_z[q, m : m + 1]
    for k in range(1, n_cross):
        z_copy(elem_z.at[cross], elem_z.at[cross], ez_send, ez_recv, k).wait_send()
    each_reach(lambda m: reach_out(elem_out, elem_in, er_send, er_recv, m), lambda c: c.start())

    apply_all(1)
    for n in range(4):
        sums[0, n : n + 1] = square(n + 1)
    copies = z_sums()
    for copy in copies:
        copy.start()
    elements(4, 5)
    total = finish_sums(copies, sums[0], got_z)
    sums[1] = total
    copies = w_sums(1)
    for copy in copies:
        copy.start()

    points = gll_points()[0]
    here = jnp.where(sub < 4, 1.0, 0.0)

    def restrict(n, carry):
        last = n == 4
        own_k = jnp.where(ends | last, 1.0, 0.0)
        own_j = jnp.where(last, keep_y, 0.0)
        own_i = here + jnp.where((sub == 4) & last, one_x, 0.0)
        columns = [column_ref[80 + 8 * i2 : 88 + 8 * i2] * own_i for i2 in range(2)]
        for c in range(3):
            lines = []
            for j in range(5):
                u = [held[n + 1, c * PER + j * 40 + k * 8 : c * PER + j * 40 + k * 8 + 8]
                     for k in range(5)]
                first, second = u[0], own_k * u[4]
                for k in range(1, 4):
                    part = float(points[k]) * u[k]
                    first, second = first + (u[k] - part), second + part
                lines.append((first, second))
            for k in range(2):
                first, second = lines[0][k], own_j * lines[4][k]
                for j in range(1, 4):
                    part = float(points[j]) * lines[j][k]
                    first, second = first + (lines[j][k] - part), second + part
                for j2, value in enumerate((first, second)):
                    for i2 in range(2):
                        row = j2 * 12 + i2 * 6 + c * 2 + k
                        rest[cross, n, row : row + 1] = jnp.sum(
                            value * columns[i2], axis=0, keepdims=True)
        return carry

    lax.fori_loop(0, 5, restrict, 0)
    for k in range(1, n_cross):
        z_copy(rest.at[cross], rest.at[cross], cz_send, cz_recv, k).start()

    each_reach(lambda m: reach_back(elem_out, elem_in, er_send, er_recv, m), lambda c: c.wait_recv())
    for m, by in enumerate(REACH):
        if by >= -HOME:
            elem_c[pl.ds(HOME + by, 16, stride=8)] = elem_in[m]
    elem_c[pl.ds(HOME, 16, stride=8)] = elem_out[...]
    for q in range(4):
        at = (12 + q) * 8
        elem_c[at : at + 8] = jnp.where(sub < 7, elem_c[at : at + 8], 0.0)
    each_reach(lambda m: reach_out(elem_out, elem_in, er_send, er_recv, m), lambda c: c.wait_send())

    total = finish_sums(copies, sums[1], got_w.at[0])
    norms = jnp.sum(total, axis=1, keepdims=True)
    largest = jnp.broadcast_to(estimate([norms[n : n + 1] for n in range(4)]), (1, LANES))
    step_poly, rest_poly = smoothing(largest, FINE_RATIO)

    for k in range(1, n_cross):
        z_copy(rest.at[from_z(k)], rest.at[from_z(k)], cz_send, cz_recv, k).wait_recv()
    blocks = []
    for q in range(4):
        value = rest_poly[0] * rest[q, 0]
        for n in range(1, 5):
            value = value + rest_poly[n] * rest[q, n]
        blocks.append(value)
    for k in range(1, n_cross):
        z_copy(rest.at[cross], rest.at[cross], cz_send, cz_recv, k).wait_send()
    nothing = jnp.zeros((12, LANES), f32)
    for q in range(4):
        before = blocks[q - 1][12:24] if q > 0 else nothing
        swapped = pltpu.roll(jnp.where(spread_to(low, 12), blocks[q][12:24], before), 64, 1)
        value = blocks[q][0:12] + swapped
        for i2 in range(2):
            coarse_out[i2 * 24 + q * 6 : i2 * 24 + q * 6 + 6] = value[i2 * 6 : i2 * 6 + 6]
    each_reach(lambda m: reach_out(coarse_out, reach_in, cr_send, cr_recv, m), lambda c: c.start())

    def add_steps(c, carry):
        at = pl.ds(pl.multiple_of(c * PER, 8), PER)
        value = held[0, at]
        for n in range(4):
            value = value + step_poly[n] * held[n + 1, at]
        held[0, at] = value
        return carry

    lax.fori_loop(0, 3, add_steps, 0)
    each_reach(lambda m: reach_back(coarse_out, reach_in, cr_send, cr_recv, m), lambda c: c.wait_recv())

    vertex[0, pl.ds(HOME, 24, stride=8)] = coarse_out[0:24]
    vertex[0, pl.ds(HOME + 1, 24, stride=8)] = coarse_out[24:48]
    for first in (True, False):
        for m, by in enumerate(REACH):
            s = HOME + by if first else HOME + 1 + by
            if 0 <= s < 8:
                part = reach_in[m, 0:24] if first else reach_in[m, 24:48]
                vertex[0, pl.ds(s, 24, stride=8)] = vertex[0, pl.ds(s, 24, stride=8)] + part
    each_reach(lambda m: reach_out(coarse_out, reach_in, cr_send, cr_recv, m), lambda c: c.wait_send())
    free = jnp.where(wide - HOME + sub < n_wide, 1.0, 0.0)

    def close(n, q):
        for c in range(3):
            at = (q * 6 + c * 2) * 8
            first, last = gather[pl.ds(at, 8)], gather[pl.ds(at + 8, 8)]
            first = first + jnp.where(inner, pltpu.roll(last, 1, 1), 0.0)
            vertex[n, pl.ds(at, 8)] = first * free
            vertex[n, pl.ds(at + 8, 8)] = free * jnp.where(outer, pltpu.roll(first, 127, 1), last)

    def close_all(n):
        lax.fori_loop(0, 4, lambda q, carry: (close(n, pl.multiple_of(q, 1)), carry)[1], 0)

    gather[...] = vertex[0]
    close_all(0)

    def coarse_step(n, carry):
        gather[...] = jnp.zeros_like(gather)

        def column(q, inside):
            base = pl.multiple_of(q * 48, 8)

            def at(c, k, up=0):
                return pl.ds(pl.multiple_of(base + (c * 16 + k * 8 + up * 48), 8), 8)

            def data(m):
                return elem_c[pl.ds(pl.multiple_of(m * 32 + q * 8, 8), 8)]

            fib = [data(0), data(1), data(2)]
            stiff = data(3)
            mass = jnp.where(stiff > 0.0, 0.125 * MASS_COEF, 0.0)
            scale = 0.125 * stiff
            grads, values = [], []
            for c in range(3):
                u = [[None, None], [None, None]]
                for k in range(2):
                    w = vertex[n, at(c, k), :]
                    u[0][k] = w
                    u[1][k] = pltpu.roll(jnp.where(low, vertex[n, at(c, k, 1), :], w), 64, 1)
                x = [[to_gauss(u[j][k], pltpu.roll(u[j][k], 7, 0)) for k in range(2)] for j in range(2)]
                gx = [[None, None], [None, None]]
                halves = [to_gauss(x[0][k][2], x[1][k][2]) for k in range(2)]
                for qj in range(2):
                    gx[qj] = to_gauss(halves[0][qj], halves[1][qj])[:2]
                gy, gz = [None, None], [[None, None], [None, None]]
                v = [[[None, None], [None, None]], [[None, None], [None, None]]]
                for qi in range(2):
                    y = [to_gauss(x[0][k][qi], x[1][k][qi]) for k in range(2)]
                    gy[qi] = to_gauss(y[0][2], y[1][2])[:2]
                    for qj in range(2):
                        v[qj][0][qi], v[qj][1][qi], gz[qj][qi] = to_gauss(y[0][qj], y[1][qj])
                grads.append((gx, gy, gz))
                values.append(v)
            part = {}
            for qj in range(2):
                for qk in range(2):
                    for qi in range(2):
                        g = [[gx[qj][qk], gy[qi][qk], gz[qj][qi]] for gx, gy, gz in grads]
                        part[qj, qk, qi] = stresses(g, fib, scale)
            for c in range(3):
                pair = ((0, 0), (0, 1), (1, 0), (1, 1))
                y = {}
                for qj, qi in pair:
                    y[qj, qi] = from_gauss(
                        mass * values[c][qj][0][qi], mass * values[c][qj][1][qi],
                        part[qj, 0, qi][c, 2] + part[qj, 1, qi][c, 2])
                x = {}
                for qi in range(2):
                    tilt = from_gauss(*[
                        part[0, qk, qi][c, 1] + part[1, qk, qi][c, 1] for qk in range(2)])
                    for k in range(2):
                        x[0, k, qi], x[1, k, qi] = from_gauss(y[0, qi][k], y[1, qi][k], tilt[k])
                half = [
                    from_gauss(*[part[qj, qk, 0][c, 0] + part[qj, qk, 1][c, 0] for qk in range(2)])
                    for qj in range(2)
                ]
                for k in range(2):
                    steep = from_gauss(half[0][k], half[1][k])
                    w = []
                    for j in range(2):
                        first, last = from_gauss(x[j, k, 0], x[j, k, 1], steep[j])
                        w.append(first + pltpu.roll(last, 1, 0))
                    other = pltpu.roll(w[1], 64, 1)
                    gather[at(c, k), :] = gather[at(c, k), :] + w[0] + jnp.where(low, 0.0, other)
                    gather[at(c, k, 1), :] = jnp.where(low, other, 0.0)
            return inside

        lax.fori_loop(0, 4, column, 0)
        close_all(n + 1)
        return carry

    lax.fori_loop(0, 3, coarse_step, 0)

    def coarse_square(n):
        total = jnp.zeros((8, LANES), f32)
        tail = jnp.zeros((8, LANES), f32)
        for m in range(12):
            first, last = vertex[n, m * 16 : m * 16 + 8], vertex[n, m * 16 + 8 : m * 16 + 16]
            total = total + first * first
            tail = tail + last * last
        return (total + jnp.where(ends, tail, 0.0))[HOME : HOME + 1]

    for n in range(4):
        sums[2, n : n + 1] = coarse_square(n)
    copies = w_sums(2)
    for copy in copies:
        copy.start()
    total = finish_sums(copies, sums[2], got_w.at[1])
    norms = jnp.sum(total, axis=1, keepdims=True)
    coarse_largest = jnp.broadcast_to(estimate([norms[n : n + 1] for n in range(4)]), (1, LANES))
    coarse_poly, _ = smoothing(coarse_largest, COARSE_RATIO)
    left, right = column_ref[80:88], column_ref[88:96]
    for c in range(3):
        ends_k = []
        for k in range(2):
            w = []
            for up in range(2):
                at = pl.ds(pl.multiple_of((cross + up) * 48, 8) + (c * 16 + k * 8), 8)
                value = coarse_poly[0] * vertex[0, at]
                for n in range(1, 4):
                    value = value + coarse_poly[n] * vertex[n, at]
                w.append(value)
            ends_k.append((w[0], pltpu.roll(jnp.where(low, w[1], w[0]), 64, 1)))
        own = [ends_k[k][0][HOME : HOME + 1] for k in range(2)]
        for ey in range(2):
            a, b = own if ey == 0 else [pltpu.roll(v, 64, 1) for v in own]
            line = jnp.where(low[:1], a, pltpu.roll(b, 1, 1))
            cor_ref[c, 0, ey : ey + 1, :] = line[:, :65]
        nodes = []
        for k in range(2):
            first, last = [
                left * jnp.broadcast_to(v[HOME : HOME + 1], (8, LANES))
                + right * jnp.broadcast_to(v[HOME + 1 : HOME + 2], (8, LANES))
                for v in ends_k[k]
            ]
            step = last - first
            nodes.append(
                [first] + [first + float(points[j]) * step for j in range(1, 4)] + [last])
        for j in range(5):
            first, last = nodes[0][j], nodes[1][j]
            step = last - first
            for k in range(5):
                at = c * PER + j * 40 + k * 8
                more = first if k == 0 else last if k == 4 else first + float(points[k]) * step
                held[0, at : at + 8] = held[0, at : at + 8] + more

    apply_all(1)

    for c in range(3):
        for j in range(4):
            for k in range(5):
                at = c * PER + j * 40 + k * 8
                value = held[0, at : at + 8]
                for n in range(4):
                    value = value + step_poly[n] * held[n + 1, at : at + 8]
                planes[k, pl.ds(c * 32 + j, 4, stride=8)] = value[:4]
                planes[k, pl.ds(c * 32 + 4 + j, 4, stride=8)] = pltpu.roll(value, 64, 1)[:4]
    use = spread_to(low, 96)
    joined = jnp.concatenate(
        [jnp.where(use, planes[k], pltpu.roll(planes[k + 1], 64, 1)) for k in (0, 2)], 1)
    row = lax.broadcasted_iota(jnp.int32, (256, 256), 0)
    z_at = lax.broadcasted_iota(jnp.int32, (256, 256), 1)
    spread = jnp.where(z_at == 4 * lax.rem(row, 64) + row // 64, 1.0, 0.0)
    out_ref[:, :, :, 0:256] = dot(joined, spread).reshape(3, 4, 8, 256)
    out_ref[:, :, :, 256:257] = planes[4][:, 63:64].reshape(3, 4, 8, 1)


def fibre_vectors(index):
    angle = index.astype(jnp.float32) * (2.0 * math.pi / NFIB)
    tilt = 0.4 * jnp.sin(3.0 * angle)
    return jnp.stack(
        [jnp.cos(angle) * jnp.cos(tilt), jnp.sin(angle) * jnp.cos(tilt), jnp.sin(tilt)]
    )


def on_device(rhs, start, stiffness, fibre_index):
    fibre = fibre_vectors(fibre_index).reshape(3, LANES)
    elem = jnp.concatenate([fibre, stiffness.reshape(1, LANES), jnp.zeros((4, LANES))], 0)
    operands = [start, rhs, elem] + tables()
    vmem = pl.BlockSpec(memory_space=pltpu.VMEM)
    f32 = jnp.float32

    def room(*shape):
        return pltpu.VMEM(shape, f32)

    def flags(*shape):
        return pltpu.SemaphoreType.DMA(shape)

    return pl.pallas_call(
        kernel,
        out_shape=(
            jax.ShapeDtypeStruct(rhs.shape, f32),
            jax.ShapeDtypeStruct((3, 1, 2, 65), f32),
        ),
        in_specs=[vmem] * len(operands),
        out_specs=(vmem, vmem),
        scratch_shapes=[
            room(6, ROWS, LANES),
            room(ROWS, LANES),
            room(PER, LANES),
            room(ROWS, LANES),
            room(ROWS, LANES),
            room(ROWS, LANES),
            room(5, 96, LANES),
            room(2, 2, FACE_X, LANES),
            room(2, 2, FACE_Y, LANES),
            room(2, 4, EDGE, LANES),
            room(2, 2, FACE_X, LANES),
            room(2, 2, FACE_Y, LANES),
            room(2, 4, EDGE, LANES),
            room(4, 5, 24, LANES),
            room(48, LANES),
            room(8, 48, LANES),
            room(4, 8, LANES),
            room(16, LANES),
            room(8, 16, LANES),
            room(128, LANES),
            room(4, 240, LANES),
            room(240, LANES),
            room(3, 8, LANES),
            room(3, 8, LANES),
            room(2, 31, 8, LANES),
            flags(2, 8), flags(2, 8),
            flags(3), flags(3),
            flags(2, 31), flags(2, 31),
            flags(3), flags(3),
            flags(3), flags(3),
            flags(8), flags(8),
            flags(8), flags(8),
        ],
        compiler_params=pltpu.CompilerParams(
            collective_id=0, has_side_effects=True, vmem_limit_bytes=32 * 1024 * 1024
        ),
    )(*operands)


def solution(mesh):
    in_specs = (
        P(None, "wide", "cross", None),
        P(None, "wide", "cross", None),
        P("wide", "cross", None),
        P("wide", "cross", None),
    )
    out_specs = (P(None, "wide", "cross", None), P(None, "wide", "cross", None))
    return jax.shard_map(
        on_device, mesh=mesh, in_specs=in_specs, out_specs=out_specs, check_vma=False
    )
```

```python
import functools
import math

import jax
import jax.numpy as jnp
import numpy as np
from jax import lax
from jax.experimental import pallas as pl
from jax.experimental.pallas import tpu as pltpu
from jax.sharding import PartitionSpec as P

NFIB = 64
LAMBDA_COEF = 2.0
SHEAR_CROSS = 1.0
SHEAR_ALONG = 3.0
FIBRE_COEF = 20.0
MASS_COEF = 0.02
FINE_RATIO = 10.0
COARSE_RATIO = 30.0

MESH = pl.DeviceIdType.MESH
LANES = 128
PER = 200
ROWS = 3 * PER
NEIGHBOURS = ((-1, 0), (1, 0), (0, -1), (0, 1), (-1, -1), (-1, 1), (1, -1), (1, 1))
FACE_X, FACE_Y, EDGE = 80, 64, 24
REACH = (-4, -3, -2, -1, 1, 2, 3, 4)
HOME = 3
FAR_FIRST = sorted(range(31), key=lambda k: -min(k + 1, 31 - k))
TOP_SELF = LAMBDA_COEF + 4.0 * SHEAR_CROSS + (SHEAR_ALONG - SHEAR_CROSS)
TOP_ALONG = 5.0 * (SHEAR_ALONG - SHEAR_CROSS) + FIBRE_COEF


def gll_points():
    root = math.sqrt(3.0 / 7.0)
    points = (np.array([-1.0, -root, 0.0, root, 1.0]) + 1.0) / 2.0
    weights = np.array([0.1, 49.0 / 90.0, 32.0 / 45.0, 49.0 / 90.0, 0.1]) / 2.0
    return (points, weights)


def lagrange_slopes(points, where):
    count = len(points)
    table = np.zeros((len(where), count))
    for i, spot in enumerate(where):
        for j in range(count):
            total = 0.0
            for k in range(count):
                if k == j:
                    continue
                term = 1.0 / (points[j] - points[k])
                for m in range(count):
                    if m != j and m != k:
                        term = term * (spot - points[m]) / (points[j] - points[m])
                total = total + term
            table[i, j] = total
    return table


def tables():
    points, weights = gll_points()
    slopes = lagrange_slopes(points, points)
    cube = np.zeros((5, 5, 8))
    cube[..., :5] = weights[:, None, None] * weights[None, :, None] * weights[None, None, :]
    columns = np.zeros((12, 8, LANES))
    columns[0:5, :5] = slopes.T[:, :, None]
    columns[5:10, :5] = slopes[:, :, None]
    columns[10, :5] = (1.0 - points)[:, None]
    columns[11, :5] = points[:, None]
    columns = columns.reshape(96, LANES)
    angle = np.arange(NFIB) * (2.0 * math.pi / NFIB)
    tilt = 0.4 * np.sin(3.0 * angle)
    fibre = np.zeros((8, LANES))
    fibre[:3, :NFIB] = [np.cos(angle) * np.cos(tilt), np.sin(angle) * np.cos(tilt), np.sin(tilt)]
    parts = (
        np.broadcast_to(cube.reshape(-1)[:, None], (PER, LANES)),
        np.concatenate([columns, fibre], 0),
    )
    return [jnp.asarray(np.ascontiguousarray(part), dtype=jnp.float32) for part in parts]


def dot(a, b):
    return jnp.dot(
        a, b, precision=lax.Precision.HIGHEST, preferred_element_type=jnp.float32
    )


def selected(values, pick):
    rows = values.shape[0]
    high = values.astype(jnp.bfloat16)
    left = values - high.astype(jnp.float32)
    middle = left.astype(jnp.bfloat16)
    low = (left - middle.astype(jnp.float32)).astype(jnp.bfloat16)
    out = jnp.dot(
        jnp.concatenate([high, middle, low], 0), pick, preferred_element_type=jnp.float32)
    return (out[:rows] + out[rows : 2 * rows]) + out[2 * rows :]


def along_line(u, table):
    half = lambda i, j: 0.5 * (float(table[i, j]) + float(table[i, 4 - j]))
    odd_half = lambda i, j: 0.5 * (float(table[i, j]) - float(table[i, 4 - j]))
    even = [u[0] + u[4], u[1] + u[3]]
    odd = [u[0] - u[4], u[1] - u[3]]
    p = [
        half(i, 0) * even[0] + half(i, 1) * even[1] + float(table[i, 2]) * u[2] for i in range(2)
    ]
    q = [odd_half(i, 0) * odd[0] + odd_half(i, 1) * odd[1] for i in range(3)]
    return [q[0] + p[0], q[1] + p[1], q[2], q[1] - p[1], q[0] - p[0]]


def plus(*terms):
    total = None
    for term in terms:
        if term is not None:
            total = term if total is None else total + term
    return total


def times(a, b):
    return None if a is None or b is None else a * b


def stresses(grad, fibre, scale):
    twice = {}
    for i in range(3):
        for j in range(i, 3):
            twice[i, j] = twice[j, i] = (
                times(grad[i][i], 2.0) if i == j else plus(grad[i][j], grad[j][i]))
    trace = times(plus(grad[0][0], grad[1][1], grad[2][2]), LAMBDA_COEF)
    along = [plus(*[times(twice[i, j], fibre[j]) for j in range(3)]) for i in range(3)]
    stretch = plus(*[times(along[i], fibre[i]) for i in range(3)])
    half = (0.25 * FIBRE_COEF) * stretch
    cross = SHEAR_ALONG - SHEAR_CROSS
    pull = [cross * along[i] + half * fibre[i] for i in range(3)]
    out = {}
    for i in range(3):
        for j in range(i, 3):
            value = plus(
                times(twice[i, j], SHEAR_CROSS) if SHEAR_CROSS != 1.0 else twice[i, j],
                fibre[i] * pull[j] + pull[i] * fibre[j] if i != j else (2.0 * fibre[i]) * pull[i],
                trace if i == j else None)
            out[i, j] = out[j, i] = value * scale
    return out


def estimate(n):
    scale = 1.0 / jnp.sqrt(n[0] + 1e-6)
    last = None
    for k in range(1, 4):
        last = jnp.sqrt((n[k] * scale) * scale + 1e-6)
        scale = scale / last
    return last


def smoothing(largest, ratio):
    upper = 1.1 * largest
    lower = upper / ratio
    centre = 0.5 * (upper + lower)
    radius = 0.5 * (upper - lower)
    spread = centre / radius
    weight = 1.0 / spread
    step = [1.0 / centre]
    rest = [jnp.ones_like(largest)]
    total = [jnp.zeros_like(largest)] * 4

    def entry(poly, n):
        return poly[n] if n < len(poly) else jnp.zeros_like(largest)

    for k in range(4):
        total = [total[n] + entry(step, n) for n in range(4)]
        rest = [entry(rest, n) - (step[n - 1] if n > 0 else 0.0) for n in range(k + 2)]
        if k < 3:
            new = 1.0 / (2.0 * spread - weight)
            step = [
                new * weight * entry(step, n) + 2.0 * new / radius * rest[n] for n in range(k + 2)
            ]
            weight = new
    return total, rest


def kernel(
    start_hbm, rhs_hbm, stiff_hbm, index_hbm, weight_hbm, column_hbm,
    out_ref, last_ref, cor_ref,
    start_ref, rhs_ref, stiff_ref, index_ref, weight_ref, column_ref, elem_ref,
    held, load, mass_w, slope_y, flux_x, flux_y, planes,
    send_x, send_y, send_e, got_x, got_y, got_e,
    rest, coarse_out, tails, tail_in, reach_in, elem_z, elem_out, elem_in, elem_c, vertex, gather,
    sums, norms, got_z, got_w,
    send_sem, recv_sem, z_send, z_recv, w_send, w_recv, ez_send, ez_recv, cz_send, cz_recv,
    er_send, er_recv, cr_send, cr_recv, in_sem, greeting,
):
    wide, cross = lax.axis_index("wide"), lax.axis_index("cross")
    n_wide, n_cross = lax.axis_size("wide"), lax.axis_size("cross")
    f32 = jnp.float32

    def within(at, by, size):
        return at >= -by if by < 0 else at < size - by

    def present(n):
        dx, dy = NEIGHBOURS[n]
        inside = None
        for here, by, size in ((wide, dx, n_wide), (cross, dy, n_cross)):
            if by:
                ok = within(here, by, size)
                inside = ok if inside is None else inside & ok
        return inside

    def place(n):
        dx, dy = NEIGHBOURS[n]
        return (wide + dx, cross + dy)

    def opposite(n):
        dx, dy = NEIGHBOURS[n]
        return NEIGHBOURS.index((-dx, -dy))

    z_peers = [(wide, lax.rem(cross + k, n_cross)) for k in range(1, n_cross)]
    w_peers = [(lax.rem(wide + k, n_wide), cross) for k in range(1, n_wide)]

    loads = [
        pltpu.make_async_copy(source, target, in_sem.at[n])
        for n, (source, target) in enumerate((
            (start_hbm, start_ref), (stiff_hbm, stiff_ref), (index_hbm, index_ref),
            (column_hbm, column_ref), (weight_hbm, weight_ref), (rhs_hbm, rhs_ref)))
    ]
    for copy in loads:
        copy.start()

    got_x[...] = jnp.zeros_like(got_x)
    got_y[...] = jnp.zeros_like(got_y)
    got_e[...] = jnp.zeros_like(got_e)
    reach_in[...] = jnp.zeros_like(reach_in)
    elem_in[...] = jnp.zeros_like(elem_in)
    got_z[...] = jnp.zeros_like(got_z)
    got_w[...] = jnp.zeros_like(got_w)
    barrier = pltpu.get_barrier_semaphore()
    expected = jnp.int32(0)
    for n in (4, 5, 6, 7, 0, 1, 2, 3):
        @pl.when(present(n))
        def _(n=n):
            pl.semaphore_signal(barrier, inc=1, device_id=place(n), device_id_type=MESH)
        expected = expected + present(n).astype(jnp.int32)

    lane = lax.broadcasted_iota(jnp.int32, (8, LANES), 1)
    sub = lax.broadcasted_iota(jnp.int32, (8, LANES), 0)
    spot = lax.rem(lane, 64)
    low = lane < 64
    ends = spot == 63
    one_x = jnp.where(wide < n_wide - 1, 1.0, 0.0)
    one_y = jnp.where(cross < n_cross - 1, 1.0, 0.0)
    keep_y = jnp.where(low, 1.0, one_y)

    def spread_to(mask, rows):
        return jnp.broadcast_to(mask[:1], (rows, LANES))

    send_x[...] = jnp.zeros_like(send_x)
    send_e[...] = jnp.zeros_like(send_e)
    sums[...] = jnp.zeros_like(sums)
    norms[...] = jnp.zeros_like(norms)
    vertex[...] = jnp.zeros_like(vertex)
    gather[...] = jnp.zeros_like(gather)
    tail_in[...] = jnp.zeros_like(tail_in)
    coarse_out[...] = jnp.zeros_like(coarse_out)
    z_at = lax.broadcasted_iota(jnp.int32, (256, 5 * LANES), 0)
    col = lax.broadcasted_iota(jnp.int32, (256, 5 * LANES), 1)
    pick = jnp.where(z_at == 4 * lax.rem(col, 64) + col // LANES, 1.0, 0.0).astype(jnp.bfloat16)

    def unpack(ref, into):
        nodes = selected(ref[:, :, :, 0:256].reshape(96, 256), pick)
        final = jnp.broadcast_to(ref[:, :, :, 256:257].reshape(96, 1), (96, LANES))
        for k in range(5):
            part = nodes[:, k * LANES : k * LANES + LANES]
            planes[k] = jnp.where(spread_to(ends, 96), final, part) if k == 4 else part
        into[...] = jnp.zeros_like(into)
        for c in range(3):
            for j in range(5):
                for k in range(5):
                    first = planes[k, pl.ds(c * 32 + j, 4, stride=8)]
                    if j < 4:
                        second = planes[k, pl.ds(c * 32 + 4 + j, 4, stride=8)]
                    else:
                        second = jnp.zeros((4, LANES), f32)
                    at = c * PER + j * 40 + k * 8
                    into[at : at + 4] = jnp.where(low[:4], first, second)

    loads[0].wait()
    unpack(start_ref, held.at[0])
    for copy in loads[1:5]:
        copy.wait()
    index = lax.broadcasted_iota(jnp.int32, (64, 64), 0)
    chosen = jnp.concatenate(
        [jnp.where(index_ref[0, n : n + 1, :] == index, 1.0, 0.0) for n in range(2)], 1)
    elem_ref[...] = dot(column_ref[96:104, :64], chosen)
    elem_ref[3:4, :] = jnp.concatenate([stiff_ref[0, n : n + 1, :] for n in range(2)], 1)
    mass_w[...] = weight_ref[...] * elem_ref[3:4, :]
    weight_ref[...] = MASS_COEF * weight_ref[...]
    elem_z[cross] = elem_ref[...]
    pl.semaphore_wait(barrier, expected)

    def z_copy(source, target, sem_out, sem_in, k, back=False):
        return pltpu.make_async_remote_copy(
            src_ref=source, dst_ref=target, send_sem=sem_out.at[k - 1], recv_sem=sem_in.at[k - 1],
            device_id=z_peers[k - 1], device_id_type=MESH)

    def from_z(k):
        return lax.rem(cross + n_cross - k, n_cross)

    def reach_out(source, into, sem_out, sem_in, m):
        back = REACH.index(-REACH[m])
        return pltpu.make_async_remote_copy(
            src_ref=source, dst_ref=into.at[back], send_sem=sem_out.at[m], recv_sem=sem_in.at[back],
            device_id=(wide + REACH[m], cross), device_id_type=MESH)

    def reach_back(source, into, sem_out, sem_in, m):
        return pltpu.make_async_remote_copy(
            src_ref=source, dst_ref=into.at[m], send_sem=sem_out.at[m], recv_sem=sem_in.at[m],
            device_id=(wide + REACH[m], cross), device_id_type=MESH)

    def each_reach(make, act):
        for m, by in enumerate(REACH):
            @pl.when(within(wide, by, n_wide))
            def _(m=m):
                act(make(m))

    def sides(s, n):
        if n < 2:
            return send_x.at[s, n], got_x.at[s, n], got_x.at[s, opposite(n)]
        if n < 4:
            return send_y.at[s, n - 2], got_y.at[s, n - 2], got_y.at[s, opposite(n) - 2]
        return send_e.at[s, n - 4], got_e.at[s, n - 4], got_e.at[s, opposite(n) - 4]

    def outgoing(s, n):
        source, _, target = sides(s, n)
        return pltpu.make_async_remote_copy(
            src_ref=source, dst_ref=target, send_sem=send_sem.at[s, n],
            recv_sem=recv_sem.at[s, opposite(n)], device_id=place(n), device_id_type=MESH)

    def incoming(s, n):
        source, target, _ = sides(s, n)
        return pltpu.make_async_remote_copy(
            src_ref=source, dst_ref=target, send_sem=send_sem.at[s, n],
            recv_sem=recv_sem.at[s, n], device_id=place(n), device_id_type=MESH)

    def exchange_start(t, s):
        for n in range(4, 8):
            dx, dy = NEIGHBOURS[n]
            i, j = (4 if dx > 0 else 0), (4 if dy > 0 else 0)
            for c in range(3):
                send_e[s, n - 4, c * 8 : c * 8 + 5] = held[
                    t, pl.ds(c * PER + j * 40 + i, 5, stride=8)]
        for n in (4, 5, 6, 7):
            @pl.when(present(n))
            def _(n=n):
                outgoing(s, n).start()
        for side in range(2):
            send_x[s, side, :75] = held[t, pl.ds(4 * side, 75, stride=8)]
        for n in (0, 1):
            @pl.when(present(n))
            def _(n=n):
                outgoing(s, n).start()
        for side in range(2):
            face = jnp.concatenate(
                [held[t, c * PER + side * 160 : c * PER + side * 160 + 40] for c in range(3)], 0)
            first, second = face[:64], face[64:]
            rolled = pltpu.roll(second, 64, 1)
            use = spread_to(low if side == 0 else ~low, 56)
            send_y[s, side, :56] = jnp.where(use, first[:56], rolled)
            send_y[s, side, 56:] = first[56:]
        for n in (2, 3):
            @pl.when(present(n))
            def _(n=n):
                outgoing(s, n).start()

    def exchange_finish(t, s):
        for n in (2, 3):
            @pl.when(present(n))
            def _(n=n):
                incoming(s, n).wait_recv()
        for side in range(2):
            got = got_y[s, side]
            use = spread_to(low if side == 0 else ~low, 64)
            first = jnp.where(use, pltpu.roll(got, 64, 1), 0.0)
            second = jnp.where(use[:56], got[:56], 0.0)
            more = jnp.concatenate([first, second], 0)
            for c in range(3):
                at = c * PER + side * 160
                held[t, at : at + 40] = held[t, at : at + 40] + more[c * 40 : c * 40 + 40]
        for n in (0, 1):
            @pl.when(present(n))
            def _(n=n):
                incoming(s, n).wait_recv()
        for side in range(2):
            value = held[t, pl.ds(4 * side, 75, stride=8)] + got_x[s, side, :75]
            held[t, pl.ds(4 * side, 75, stride=8)] = value
        for n in (4, 5, 6, 7):
            @pl.when(present(n))
            def _(n=n):
                incoming(s, n).wait_recv()
        for n in range(4, 8):
            dx, dy = NEIGHBOURS[n]
            i, j = (4 if dx > 0 else 0), (4 if dy > 0 else 0)
            use = low if dy < 0 else ~low
            for c in range(3):
                more = jnp.where(use, pltpu.roll(got_e[s, n - 4, c * 8 : c * 8 + 8], 64, 1), 0.0)
                at = pl.ds(c * PER + j * 40 + i, 5, stride=8)
                held[t, at] = held[t, at] + more[:5]
        for n in range(8):
            @pl.when(present(n))
            def _(n=n):
                outgoing(s, n).wait_send()

    fibre = [elem_ref[i : i + 1, :] for i in range(3)]
    slopes = lagrange_slopes(gll_points()[0], gll_points()[0])

    def across(ref, at, table):
        total = None
        for i in range(5):
            row = jnp.broadcast_to(ref[pl.ds(at + i, 1), :], (8, LANES))
            term = column_ref[(table * 5 + i) * 8 : (table * 5 + i) * 8 + 8] * row
            total = term if total is None else total + term
        return total

    def elements(t, into):
        source = held.at[t]
        target = held.at[into]
        for c in range(3):
            for k in range(5):
                at = [c * PER + j * 40 + k * 8 for j in range(5)]
                for j, v in enumerate(along_line([source[a : a + 8] for a in at], slopes)):
                    slope_y[at[j] : at[j] + 8] = v

        def layer(j, carry):
            base = pl.multiple_of(j * 40, 8)

            def at(c, k):
                return pl.ds(pl.multiple_of(base + (c * PER + k * 8), 8), 8)

            grad_z = [along_line([source[at(c, k), :] for k in range(5)], slopes) for c in range(3)]
            flux_z = [[None] * 5 for _ in range(3)]
            for k in range(5):
                g = [
                    [across(source, base + (c * PER + k * 8), 0), slope_y[at(c, k), :], grad_z[c][k]]
                    for c in range(3)
                ]
                part = stresses(g, fibre, mass_w[at(0, k), :])
                for c in range(3):
                    flux_x[at(c, k), :] = part[c, 0]
                    flux_y[at(c, k), :] = part[c, 1]
                    flux_z[c][k] = part[c, 2]
            for c in range(3):
                pull = along_line(flux_z[c], slopes.T)
                for k in range(5):
                    mass = weight_ref[at(0, k), :] * source[at(c, k), :]
                    target[at(c, k), :] = (
                        pull[k] + mass + across(flux_x, base + (c * PER + k * 8), 1))
            return carry

        lax.fori_loop(0, 5, layer, 0)
        for c in range(3):
            for k in range(5):
                at = [c * PER + j * 40 + k * 8 for j in range(5)]
                for j, v in enumerate(along_line([flux_y[a : a + 8] for a in at], slopes.T)):
                    target[at[j] : at[j] + 8] = target[at[j] : at[j] + 8] + v

    inner = spread_to(spot > 0, 8)
    outer = spread_to(spot < 63, 8)

    def gather_local(t):
        for c in range(3):
            for j in range(5):
                at = c * PER + j * 40
                first, last = held[t, at : at + 8], held[t, at + 32 : at + 40]
                held[t, at : at + 8] = first + jnp.where(inner, pltpu.roll(last, 1, 1), 0.0)
                held[t, at + 32 : at + 40] = last + jnp.where(outer, pltpu.roll(first, 127, 1), 0.0)
            at = c * PER
            first, last = held[t, at : at + 40], held[t, at + 160 : at + 200]
            use = spread_to(low, 40)
            held[t, at : at + 40] = first + jnp.where(use, 0.0, pltpu.roll(last, 64, 1))
            held[t, at + 160 : at + 200] = spread_to(keep_y, 40) * (
                last + jnp.where(use, pltpu.roll(first, 64, 1), 0.0))
        held[t, pl.ds(4, 75, stride=8)] = held[t, pl.ds(4, 75, stride=8)] * one_x

    def square(t):
        total = jnp.zeros((8, LANES), f32)
        tail = jnp.zeros((8, LANES), f32)
        for c in range(3):
            for j in range(4):
                for k in range(5):
                    at = c * PER + j * 40 + k * 8
                    v = held[t, at : at + 8]
                    if k < 4:
                        total = total + v * v
                    else:
                        tail = tail + v * v
        total = total + jnp.where(ends, tail, 0.0)
        total = jnp.where(sub < 4, total, 0.0)
        return jnp.sum(total, axis=0, keepdims=True)

    def z_sums():
        return [
            z_copy(sums.at[0, 0:1], got_z.at[k - 1 : k], z_send, z_recv, k)
            for k in range(1, n_cross)
        ]

    def w_sums(slot):
        return [
            pltpu.make_async_remote_copy(
                src_ref=sums.at[slot, 0:1], dst_ref=got_w.at[slot - 1, k : k + 1],
                send_sem=w_send.at[slot - 1, k], recv_sem=w_recv.at[slot - 1, k],
                device_id=w_peers[k], device_id_type=MESH)
            for k in FAR_FIRST
        ]

    def finish_sums(copies, own, got):
        for copy in copies:
            copy.wait_recv()
        total = own + jnp.sum(got[...], axis=0, keepdims=True)
        for copy in copies:
            copy.wait_send()
        return total

    def in_one_row(parts):
        whole = jnp.sum(parts, axis=1, keepdims=True)
        return jnp.sum(jnp.where(lane // 32 == sub, whole, 0.0), axis=0, keepdims=True)

    def out_of_row(row):
        whole = jnp.sum(jnp.where(lane == 32 * sub, row, 0.0), axis=1, keepdims=True)
        return [jnp.broadcast_to(whole[n : n + 1], (1, LANES)) for n in range(4)]

    def greet(t):
        for stage in range(5):
            @pl.when(t == stage)
            def _(stage=stage):
                for side in range(2):
                    sign = (-1, 1)[side]
                    if stage > 0:
                        @pl.when(within(wide, sign * 2**stage, n_wide))
                        def _(side=side):
                            pl.semaphore_wait(greeting.at[stage - 1, side], 1)
                if stage < 4:
                    for side in range(2):
                        by = (-1, 1)[side] * 2 ** (stage + 1)

                        @pl.when(within(wide, by, n_wide))
                        def _(side=side, by=by):
                            pl.semaphore_signal(
                                greeting.at[stage, 1 - side], inc=1, device_id=(wide + by, cross),
                                device_id_type=MESH)

    def apply_all(base, squares, late=None):
        def step(t, carry):
            elements(t, t + 1)
            gather_local(t + 1)

            @pl.when(t == 0)
            def _():
                held[1] = load[...] - held[1]

            s = lax.rem(t + base, 2)
            exchange_start(t + 1, s)
            if squares:
                greet(t)
                norms[pl.ds(t, 1)] = square(t)
            if late is not None:
                @pl.when(t == 3)
                def _():
                    late()
            exchange_finish(t + 1, s)
            return carry

        lax.fori_loop(0, 4, step, 0)

    exchange_start(0, 0)
    loads[5].wait()
    unpack(rhs_ref, load)
    exchange_finish(0, 0)
    apply_all(1, True)
    norms[4:5] = square(4)
    sums[0, 0:1] = in_one_row(norms[1:9])
    copies = z_sums()
    for copy in copies:
        copy.start()
    for k in range(1, n_cross):
        z_copy(elem_z.at[cross], elem_z.at[cross], ez_send, ez_recv, k).start()
    greet(4)
    elements(4, 5)
    sums[1, 0:1] = finish_sums(copies, sums[0, 0:1], got_z)
    copies = w_sums(1)
    for copy in copies:
        copy.start()
    for k in range(1, n_cross):
        z_copy(elem_z.at[from_z(k)], elem_z.at[from_z(k)], ez_send, ez_recv, k).wait_recv()
    for q in range(4):
        for m in range(4):
            elem_out[m * 4 + q : m * 4 + q + 1] = elem_z[q, m : m + 1]
    for k in range(1, n_cross):
        z_copy(elem_z.at[cross], elem_z.at[cross], ez_send, ez_recv, k).wait_send()
    each_reach(lambda m: reach_out(elem_out, elem_in, er_send, er_recv, m), lambda c: c.start())

    points = gll_points()[0]
    here = jnp.where(sub < 4, 1.0, 0.0)

    def restrict(n, carry):
        last = n == 4
        own_k = jnp.where(ends | last, 1.0, 0.0)
        own_j = jnp.where(last, keep_y, 0.0)
        own_i = here + jnp.where((sub == 4) & last, one_x, 0.0)
        columns = [column_ref[80 + 8 * i2 : 88 + 8 * i2] * own_i for i2 in range(2)]
        for c in range(3):
            lines = []
            for j in range(5):
                u = [held[n + 1, c * PER + j * 40 + k * 8 : c * PER + j * 40 + k * 8 + 8]
                     for k in range(5)]
                first, second = u[0], own_k * u[4]
                for k in range(1, 4):
                    part = float(points[k]) * u[k]
                    first, second = first + (u[k] - part), second + part
                lines.append((first, second))
            for k in range(2):
                first, second = lines[0][k], own_j * lines[4][k]
                for j in range(1, 4):
                    part = float(points[j]) * lines[j][k]
                    first, second = first + (lines[j][k] - part), second + part
                for j2, value in enumerate((first, second)):
                    for i2 in range(2):
                        row = j2 * 12 + i2 * 6 + c * 2 + k
                        rest[cross, n, row : row + 1] = jnp.sum(
                            value * columns[i2], axis=0, keepdims=True)
        return carry

    lax.fori_loop(0, 5, restrict, 0)
    for k in range(1, n_cross):
        z_copy(rest.at[cross], rest.at[cross], cz_send, cz_recv, k).start()

    each_reach(lambda m: reach_back(elem_out, elem_in, er_send, er_recv, m), lambda c: c.wait_recv())
    for m, by in enumerate(REACH):
        if by >= -HOME:
            elem_c[pl.ds(HOME + by, 16, stride=8)] = elem_in[m]
    elem_c[pl.ds(HOME, 16, stride=8)] = elem_out[...]
    for q in range(4):
        at = (12 + q) * 8
        elem_c[at : at + 8] = jnp.where(sub < 7, elem_c[at : at + 8], 0.0)
    each_reach(lambda m: reach_out(elem_out, elem_in, er_send, er_recv, m), lambda c: c.wait_send())

    largest = estimate(out_of_row(finish_sums(copies, sums[1, 0:1], got_w.at[0])))
    step_poly, rest_poly = smoothing(largest, FINE_RATIO)

    for k in range(1, n_cross):
        z_copy(rest.at[from_z(k)], rest.at[from_z(k)], cz_send, cz_recv, k).wait_recv()
    blocks = []
    for q in range(4):
        value = rest_poly[0] * rest[q, 0]
        for n in range(1, 5):
            value = value + rest_poly[n] * rest[q, n]
        blocks.append(value)
    for k in range(1, n_cross):
        z_copy(rest.at[cross], rest.at[cross], cz_send, cz_recv, k).wait_send()
    nothing = jnp.zeros((12, LANES), f32)
    for q in range(4):
        before = blocks[q - 1][12:24] if q > 0 else nothing
        swapped = pltpu.roll(jnp.where(spread_to(low, 12), blocks[q][12:24], before), 64, 1)
        value = blocks[q][0:12] + swapped
        moved = pltpu.roll(value, 1, 1)
        for i2 in range(2):
            for c in range(3):
                first, last = i2 * 6 + c * 2, i2 * 6 + c * 2 + 1
                row = i2 * 12 + q * 3 + c
                coarse_out[row : row + 1] = value[first : first + 1] + jnp.where(
                    inner[:1], moved[last : last + 1], 0.0)
                tails[row : row + 1] = value[last : last + 1]
    late = pltpu.roll(
        jnp.where(spread_to(ends, 24), tails[...], 0.0), 1, 1, stride=1, stride_axis=0)
    coarse_out[24:25] = jnp.sum(late, axis=0, keepdims=True)
    each_reach(lambda m: reach_out(coarse_out, reach_in, cr_send, cr_recv, m), lambda c: c.start())

    def add_steps(c, carry):
        at = pl.ds(pl.multiple_of(c * PER, 8), PER)
        value = held[0, at]
        for n in range(4):
            value = value + step_poly[n] * held[n + 1, at]
        held[0, at] = value
        return carry

    lax.fori_loop(0, 3, add_steps, 0)
    each_reach(lambda m: reach_back(coarse_out, reach_in, cr_send, cr_recv, m), lambda c: c.wait_recv())

    free = jnp.where(wide - HOME + sub < n_wide, 1.0, 0.0)
    for i2 in range(2):
        for by in (0,) + REACH:
            s = HOME + by + i2
            if 0 <= s < 8:
                part = coarse_out if by == 0 else reach_in.at[REACH.index(by)]
                gather[pl.ds(i2 * 96 + s, 12, stride=8)] = part[i2 * 12 : i2 * 12 + 12]
                tail_in[i2 * 8 + s : i2 * 8 + s + 1] = part[24:25]
    for m in range(12):
        first = gather[m * 8 : m * 8 + 8] + gather[96 + m * 8 : 104 + m * 8]
        last = pltpu.roll(tail_in[0:8], 127 - m, 1) + pltpu.roll(tail_in[8:16], 115 - m, 1)
        vertex[0, m * 16 : m * 16 + 8] = first * free
        vertex[0, m * 16 + 8 : m * 16 + 16] = free * jnp.where(
            outer, pltpu.roll(first, 127, 1), last)
    each_reach(lambda m: reach_out(coarse_out, reach_in, cr_send, cr_recv, m), lambda c: c.wait_send())

    def close(n, q):
        for c in range(3):
            at = (q * 6 + c * 2) * 8
            first, last = gather[pl.ds(at, 8)], gather[pl.ds(at + 8, 8)]
            first = first + jnp.where(inner, pltpu.roll(last, 1, 1), 0.0)
            vertex[n, pl.ds(at, 8)] = first * free
            vertex[n, pl.ds(at + 8, 8)] = free * jnp.where(outer, pltpu.roll(first, 127, 1), last)

    def close_all(n):
        for q in range(4):
            close(n, q)

    def coarse_step(n, carry):
        carried = {}

        def column(q):
            def at(c, k, up=0):
                return pl.ds((q + up) * 48 + c * 16 + k * 8, 8)

            def data(m):
                return elem_c[m * 32 + q * 8 : m * 32 + q * 8 + 8]

            fib = [data(0), data(1), data(2)]
            stiff = data(3)
            mass = jnp.where(stiff > 0.0, MASS_COEF, 0.0)
            modes = []
            for c in range(3):
                m = {}
                for k in range(2):
                    w = vertex[n, at(c, k), :]
                    beside = pltpu.roll(jnp.where(low, vertex[n, at(c, k, 1), :], w), 64, 1)
                    for b, v in enumerate((w + beside, beside - w)):
                        after = pltpu.roll(v, 7, 0)
                        m[0, b, k], m[1, b, k] = v + after, after - v
                modes.append({})
                for a in range(2):
                    for b in range(2):
                        first, last = m[a, b, 0], m[a, b, 1]
                        modes[c][a, b, 0], modes[c][a, b, 1] = first + last, last - first
            back = [{}, {}, {}]

            def put(c, mode, value):
                back[c][mode] = back[c][mode] + value if mode in back[c] else value

            for ones, weight in (((0, 0, 0), 16.0), ((1, 0, 0), 48.0), ((0, 1, 0), 48.0), ((0, 0, 1), 48.0)):
                at_mode = {
                    d: tuple(1 if d == e else ones[e] for e in range(3))
                    for d in range(3) if not ones[d]
                }
                grad = [
                    [modes[c][at_mode[d]] if d in at_mode else None for d in range(3)]
                    for c in range(3)
                ]
                part = stresses(grad, fib, stiff * (1.0 / weight))
                for d in at_mode:
                    for c in range(3):
                        put(c, at_mode[d], part[c, d])
            top = [modes[c][1, 1, 1] for c in range(3)]
            along = fib[0] * top[0] + fib[1] * top[1] + fib[2] * top[2]
            along = (stiff * (TOP_ALONG / 144.0)) * along
            top_scale = stiff * (TOP_SELF / 144.0)
            for c in range(3):
                put(c, (1, 1, 1), top_scale * top[c] + along * fib[c])
                for mode, value in modes[c].items():
                    count = sum(mode)
                    put(c, mode, (mass * (0.25 ** (3 - count) / 12.0**count)) * value)
                for k in range(2):
                    w = []
                    xs = {}
                    for a in range(2):
                        for b in range(2):
                            first, last = back[c][a, b, 0], back[c][a, b, 1]
                            xs[a, b] = first + last if k else first - last
                    for b in range(2):
                        w.append((xs[0, b] - xs[1, b]) + pltpu.roll(xs[0, b] + xs[1, b], 1, 0))
                    other = pltpu.roll(w[0] + w[1], 64, 1)
                    own = jnp.where(low, carried[c, k], other) if q else jnp.where(low, 0.0, other)
                    gather[at(c, k), :] = (w[0] - w[1]) + own
                    carried[c, k] = other

        for q in range(4):
            column(q)
        close_all(n + 1)
        return carry

    lax.fori_loop(0, 3, coarse_step, 0)

    def coarse_square(n):
        total = jnp.zeros((8, LANES), f32)
        tail = jnp.zeros((8, LANES), f32)
        for m in range(12):
            first, last = vertex[n, m * 16 : m * 16 + 8], vertex[n, m * 16 + 8 : m * 16 + 16]
            total = total + first * first
            tail = tail + last * last
        return (total + jnp.where(ends, tail, 0.0))[HOME : HOME + 1]

    for n in range(4):
        norms[n : n + 1] = coarse_square(n)
    sums[2, 0:1] = in_one_row(norms[0:8])
    copies = w_sums(2)
    for copy in copies:
        copy.start()
    coarse_largest = estimate(out_of_row(finish_sums(copies, sums[2, 0:1], got_w.at[1])))
    coarse_poly, _ = smoothing(coarse_largest, COARSE_RATIO)
    left, right = column_ref[80:88], column_ref[88:96]
    for c in range(3):
        ends_k = []
        for k in range(2):
            w = []
            for up in range(2):
                at = pl.ds(pl.multiple_of((cross + up) * 48, 8) + (c * 16 + k * 8), 8)
                value = coarse_poly[0] * vertex[0, at]
                for n in range(1, 4):
                    value = value + coarse_poly[n] * vertex[n, at]
                w.append(value)
            ends_k.append((w[0], pltpu.roll(jnp.where(low, w[1], w[0]), 64, 1)))
        own = [ends_k[k][0][HOME : HOME + 1] for k in range(2)]
        for ey in range(2):
            a, b = own if ey == 0 else [pltpu.roll(v, 64, 1) for v in own]
            line = jnp.where(low[:1], a, pltpu.roll(b, 1, 1))
            cor_ref[c, 0, ey : ey + 1, :] = line[:, :65]
        nodes = []
        for k in range(2):
            first, last = [
                left * jnp.broadcast_to(v[HOME : HOME + 1], (8, LANES))
                + right * jnp.broadcast_to(v[HOME + 1 : HOME + 2], (8, LANES))
                for v in ends_k[k]
            ]
            step = last - first
            nodes.append(
                [first] + [first + float(points[j]) * step for j in range(1, 4)] + [last])
        for j in range(5):
            first, last = nodes[0][j], nodes[1][j]
            step = last - first
            for k in range(5):
                at = c * PER + j * 40 + k * 8
                more = first if k == 0 else last if k == 4 else first + float(points[k]) * step
                held[0, at : at + 8] = held[0, at : at + 8] + more

    row = lax.broadcasted_iota(jnp.int32, (256, 256), 0)
    z_at = lax.broadcasted_iota(jnp.int32, (256, 256), 1)
    spread = jnp.where(z_at == 4 * lax.rem(row, 64) + row // 64, 1.0, 0.0).astype(jnp.bfloat16)

    def to_nodes(value_at, ref):
        for c in range(3):
            for j in range(4):
                for k in range(5):
                    value = value_at(pl.ds(c * PER + j * 40 + k * 8, 8))
                    planes[k, pl.ds(c * 32 + j, 4, stride=8)] = value[:4]
                    planes[k, pl.ds(c * 32 + 4 + j, 4, stride=8)] = pltpu.roll(value, 64, 1)[:4]
        use = spread_to(low, 96)
        joined = jnp.concatenate(
            [jnp.where(use, planes[k], pltpu.roll(planes[k + 1], 64, 1)) for k in (0, 2)], 1)
        ref[:, :, :, 0:256] = selected(joined, spread).reshape(3, 4, 8, 256)
        ref[:, :, :, 256:257] = planes[4][:, 63:64].reshape(3, 4, 8, 1)

    def most(at):
        value = held[0, at]
        for n in range(3):
            value = value + step_poly[n] * held[n + 1, at]
        return value

    apply_all(1, False, lambda: to_nodes(most, out_ref))
    to_nodes(lambda at: step_poly[3] * held[4, at], last_ref)


def on_device(rhs, start, stiffness, fibre_index):
    operands = [start, rhs, stiffness, fibre_index] + tables()
    vmem = pl.BlockSpec(memory_space=pltpu.VMEM)
    f32 = jnp.float32

    def room(*shape):
        return pltpu.VMEM(shape, f32)

    def flags(*shape):
        return pltpu.SemaphoreType.DMA(shape)

    most, last, correction = pl.pallas_call(
        kernel,
        out_shape=(
            jax.ShapeDtypeStruct(rhs.shape, f32),
            jax.ShapeDtypeStruct(rhs.shape, f32),
            jax.ShapeDtypeStruct((3, 1, 2, 65), f32),
        ),
        in_specs=[pl.BlockSpec(memory_space=pltpu.HBM)] * len(operands),
        out_specs=(vmem, vmem, vmem),
        scratch_shapes=[
            room(3, 4, 8, 257),
            room(3, 4, 8, 257),
            room(1, 2, 64),
            pltpu.VMEM((1, 2, 64), jnp.int32),
            room(PER, LANES),
            room(104, LANES),
            room(8, LANES),
            room(6, ROWS, LANES),
            room(ROWS, LANES),
            room(PER, LANES),
            room(ROWS, LANES),
            room(ROWS, LANES),
            room(ROWS, LANES),
            room(5, 96, LANES),
            room(2, 2, FACE_X, LANES),
            room(2, 2, FACE_Y, LANES),
            room(2, 4, EDGE, LANES),
            room(2, 2, FACE_X, LANES),
            room(2, 2, FACE_Y, LANES),
            room(2, 4, EDGE, LANES),
            room(4, 5, 24, LANES),
            room(32, LANES),
            room(24, LANES),
            room(16, LANES),
            room(8, 32, LANES),
            room(4, 8, LANES),
            room(16, LANES),
            room(8, 16, LANES),
            room(128, LANES),
            room(4, 240, LANES),
            room(240, LANES),
            room(3, 8, LANES),
            room(16, LANES),
            room(8, LANES),
            room(2, 32, LANES),
            flags(2, 8), flags(2, 8),
            flags(3), flags(3),
            flags(2, 31), flags(2, 31),
            flags(3), flags(3),
            flags(3), flags(3),
            flags(8), flags(8),
            flags(8), flags(8),
            flags(6),
            pltpu.SemaphoreType.REGULAR((4, 2)),
        ],
        compiler_params=pltpu.CompilerParams(
            collective_id=0, has_side_effects=True, vmem_limit_bytes=60 * 1024 * 1024
        ),
    )(*operands)
    return most + last, correction


def solution(mesh):
    in_specs = (
        P(None, "wide", "cross", None),
        P(None, "wide", "cross", None),
        P("wide", "cross", None),
        P("wide", "cross", None),
    )
    out_specs = (P(None, "wide", "cross", None), P(None, "wide", "cross", None))
    return jax.shard_map(
        on_device, mesh=mesh, in_specs=in_specs, out_specs=out_specs, check_vma=False
    )
```

```python
import functools
import math

import jax
import jax.numpy as jnp
import numpy as np
from jax import lax
from jax.experimental import pallas as pl
from jax.experimental.pallas import tpu as pltpu
from jax.sharding import PartitionSpec as P

NFIB = 64
LAMBDA_COEF = 2.0
SHEAR_CROSS = 1.0
SHEAR_ALONG = 3.0
FIBRE_COEF = 20.0
MASS_COEF = 0.02
FINE_RATIO = 10.0
COARSE_RATIO = 30.0

MESH = pl.DeviceIdType.MESH
LANES = 128
PER = 200
ROWS = 3 * PER
NEIGHBOURS = ((-1, 0), (1, 0), (0, -1), (0, 1), (-1, -1), (-1, 1), (1, -1), (1, 1))
FACE_X, FACE_Y, EDGE = 80, 64, 24
REACH = (-4, -3, -2, -1, 1, 2, 3, 4)
HOME = 3
FAR_FIRST = sorted(range(31), key=lambda k: -min(k + 1, 31 - k))
TOP_SELF = LAMBDA_COEF + 4.0 * SHEAR_CROSS + (SHEAR_ALONG - SHEAR_CROSS)
TOP_ALONG = 5.0 * (SHEAR_ALONG - SHEAR_CROSS) + FIBRE_COEF


def gll_points():
    root = math.sqrt(3.0 / 7.0)
    points = (np.array([-1.0, -root, 0.0, root, 1.0]) + 1.0) / 2.0
    weights = np.array([0.1, 49.0 / 90.0, 32.0 / 45.0, 49.0 / 90.0, 0.1]) / 2.0
    return (points, weights)


def lagrange_slopes(points, where):
    count = len(points)
    table = np.zeros((len(where), count))
    for i, spot in enumerate(where):
        for j in range(count):
            total = 0.0
            for k in range(count):
                if k == j:
                    continue
                term = 1.0 / (points[j] - points[k])
                for m in range(count):
                    if m != j and m != k:
                        term = term * (spot - points[m]) / (points[j] - points[m])
                total = total + term
            table[i, j] = total
    return table


def tables():
    points, weights = gll_points()
    slopes = lagrange_slopes(points, points)
    cube = np.zeros((5, 5, 8))
    cube[..., :5] = weights[:, None, None] * weights[None, :, None] * weights[None, None, :]
    columns = np.zeros((12, 8, LANES))
    columns[0:5, :5] = slopes.T[:, :, None]
    columns[5:10, :5] = slopes[:, :, None]
    columns[10, :5] = (1.0 - points)[:, None]
    columns[11, :5] = points[:, None]
    columns = columns.reshape(96, LANES)
    angle = np.arange(NFIB) * (2.0 * math.pi / NFIB)
    tilt = 0.4 * np.sin(3.0 * angle)
    fibre = np.zeros((8, LANES))
    fibre[:3, :NFIB] = [np.cos(angle) * np.cos(tilt), np.sin(angle) * np.cos(tilt), np.sin(tilt)]
    parts = (
        np.broadcast_to(cube.reshape(-1)[:, None], (PER, LANES)),
        np.concatenate([columns, fibre], 0),
    )
    return [jnp.asarray(np.ascontiguousarray(part), dtype=jnp.float32) for part in parts]


def dot(a, b):
    return jnp.dot(
        a, b, precision=lax.Precision.HIGHEST, preferred_element_type=jnp.float32
    )


def selected(values, pick):
    rows = values.shape[0]
    high = values.astype(jnp.bfloat16)
    left = values - high.astype(jnp.float32)
    middle = left.astype(jnp.bfloat16)
    low = (left - middle.astype(jnp.float32)).astype(jnp.bfloat16)
    out = jnp.dot(
        jnp.concatenate([high, middle, low], 0), pick, preferred_element_type=jnp.float32)
    return (out[:rows] + out[rows : 2 * rows]) + out[2 * rows :]


def along_line(u, table):
    half = lambda i, j: 0.5 * (float(table[i, j]) + float(table[i, 4 - j]))
    odd_half = lambda i, j: 0.5 * (float(table[i, j]) - float(table[i, 4 - j]))
    even = [u[0] + u[4], u[1] + u[3]]
    odd = [u[0] - u[4], u[1] - u[3]]
    p = [
        half(i, 0) * even[0] + half(i, 1) * even[1] + float(table[i, 2]) * u[2] for i in range(2)
    ]
    q = [odd_half(i, 0) * odd[0] + odd_half(i, 1) * odd[1] for i in range(3)]
    return [q[0] + p[0], q[1] + p[1], q[2], q[1] - p[1], q[0] - p[0]]


def plus(*terms):
    total = None
    for term in terms:
        if term is not None:
            total = term if total is None else total + term
    return total


def times(a, b):
    return None if a is None or b is None else a * b


def stresses(grad, fibre, scale):
    twice = {}
    for i in range(3):
        for j in range(i, 3):
            twice[i, j] = twice[j, i] = (
                times(grad[i][i], 2.0) if i == j else plus(grad[i][j], grad[j][i]))
    trace = times(plus(grad[0][0], grad[1][1], grad[2][2]), LAMBDA_COEF)
    along = [plus(*[times(twice[i, j], fibre[j]) for j in range(3)]) for i in range(3)]
    stretch = plus(*[times(along[i], fibre[i]) for i in range(3)])
    half = (0.25 * FIBRE_COEF) * stretch
    cross = SHEAR_ALONG - SHEAR_CROSS
    pull = [cross * along[i] + half * fibre[i] for i in range(3)]
    out = {}
    for i in range(3):
        for j in range(i, 3):
            value = plus(
                times(twice[i, j], SHEAR_CROSS) if SHEAR_CROSS != 1.0 else twice[i, j],
                fibre[i] * pull[j] + pull[i] * fibre[j] if i != j else (2.0 * fibre[i]) * pull[i],
                trace if i == j else None)
            out[i, j] = out[j, i] = value * scale
    return out


def estimate(n):
    scale = 1.0 / (n[0] + 1e-6)
    for k in range(1, 3):
        scale = scale / (n[k] * scale + 1e-6)
    return jnp.sqrt(n[3] * scale + 1e-6)


def smoothing(largest, ratio):
    upper = 1.1
    lower = upper / ratio
    centre, radius = 0.5 * (upper + lower), 0.5 * (upper - lower)
    spread = centre / radius
    weight = 1.0 / spread
    step = np.array([1.0 / centre, 0.0, 0.0, 0.0, 0.0])
    rest = np.array([1.0, 0.0, 0.0, 0.0, 0.0])
    total = np.zeros(5)
    for k in range(4):
        total = total + step
        rest = rest - np.concatenate([[0.0], step[:4]])
        if k < 3:
            new = 1.0 / (2.0 * spread - weight)
            step = new * weight * step + 2.0 * new / radius * rest
            weight = new
    inverse = 1.0 / largest
    powers = [None, inverse]
    for n in range(2, 5):
        powers.append(powers[-1] * inverse)
    rests = [float(rest[n]) * (powers[n] if n else jnp.ones_like(largest)) for n in range(5)]
    return [float(total[n]) * powers[n + 1] for n in range(4)], rests


def kernel(
    start_hbm, rhs_hbm, stiff_hbm, index_hbm, weight_hbm, column_hbm,
    out_ref, last_ref, cor_ref,
    start_ref, rhs_ref, stiff_ref, index_ref, weight_ref, column_ref, elem_ref,
    held, load, mass_w, slope_y, flux_x, flux_y, planes,
    send_x, send_y, send_e, got_x, got_y, got_e,
    rest, coarse_out, tails, tail_in, reach_in, elem_z, elem_out, elem_in, elem_c, vertex, gather,
    sums, norms, got_z, got_w,
    send_sem, recv_sem, sum_send, sum_recv, ez_send, ez_recv, cz_send, cz_recv,
    er_send, er_recv, cr_send, cr_recv, in_sem, greeting,
):
    wide, cross = lax.axis_index("wide"), lax.axis_index("cross")
    n_wide, n_cross = lax.axis_size("wide"), lax.axis_size("cross")
    f32 = jnp.float32

    def within(at, by, size):
        return at >= -by if by < 0 else at < size - by

    def present(n):
        dx, dy = NEIGHBOURS[n]
        inside = None
        for here, by, size in ((wide, dx, n_wide), (cross, dy, n_cross)):
            if by:
                ok = within(here, by, size)
                inside = ok if inside is None else inside & ok
        return inside

    def place(n):
        dx, dy = NEIGHBOURS[n]
        return (wide + dx, cross + dy)

    def opposite(n):
        dx, dy = NEIGHBOURS[n]
        return NEIGHBOURS.index((-dx, -dy))

    z_peers = [(wide, lax.rem(cross + k, n_cross)) for k in range(1, n_cross)]
    w_peers = [(lax.rem(wide + k, n_wide), cross) for k in range(1, n_wide)]

    loads = [
        pltpu.make_async_copy(source, target, in_sem.at[n])
        for n, (source, target) in enumerate((
            (start_hbm, start_ref), (stiff_hbm, stiff_ref), (index_hbm, index_ref),
            (column_hbm, column_ref), (weight_hbm, weight_ref), (rhs_hbm, rhs_ref)))
    ]
    for copy in loads:
        copy.start()

    got_x[...] = jnp.zeros_like(got_x)
    got_y[...] = jnp.zeros_like(got_y)
    got_e[...] = jnp.zeros_like(got_e)
    reach_in[...] = jnp.zeros_like(reach_in)
    elem_in[...] = jnp.zeros_like(elem_in)
    got_z[...] = jnp.zeros_like(got_z)
    got_w[...] = jnp.zeros_like(got_w)
    barrier = pltpu.get_barrier_semaphore()
    expected = jnp.int32(0)
    for n in (4, 5, 6, 7, 0, 1, 2, 3):
        @pl.when(present(n))
        def _(n=n):
            pl.semaphore_signal(barrier, inc=1, device_id=place(n), device_id_type=MESH)
        expected = expected + present(n).astype(jnp.int32)

    lane = lax.broadcasted_iota(jnp.int32, (8, LANES), 1)
    sub = lax.broadcasted_iota(jnp.int32, (8, LANES), 0)
    spot = lax.rem(lane, 64)
    low = lane < 64
    ends = spot == 63
    one_x = jnp.where(wide < n_wide - 1, 1.0, 0.0)
    one_y = jnp.where(cross < n_cross - 1, 1.0, 0.0)
    keep_y = jnp.where(low, 1.0, one_y)

    def spread_to(mask, rows):
        return jnp.broadcast_to(mask[:1], (rows, LANES))

    send_x[...] = jnp.zeros_like(send_x)
    send_e[...] = jnp.zeros_like(send_e)
    sums[...] = jnp.zeros_like(sums)
    norms[...] = jnp.zeros_like(norms)
    vertex[...] = jnp.zeros_like(vertex)
    gather[...] = jnp.zeros_like(gather)
    tail_in[...] = jnp.zeros_like(tail_in)
    coarse_out[...] = jnp.zeros_like(coarse_out)
    z_at = lax.broadcasted_iota(jnp.int32, (256, 5 * LANES), 0)
    col = lax.broadcasted_iota(jnp.int32, (256, 5 * LANES), 1)
    pick = jnp.where(z_at == 4 * lax.rem(col, 64) + col // LANES, 1.0, 0.0).astype(jnp.bfloat16)

    def unpack(ref, into):
        nodes = selected(ref[:, :, :, 0:256].reshape(96, 256), pick)
        final = jnp.broadcast_to(ref[:, :, :, 256:257].reshape(96, 1), (96, LANES))
        for k in range(5):
            part = nodes[:, k * LANES : k * LANES + LANES]
            planes[k] = jnp.where(spread_to(ends, 96), final, part) if k == 4 else part
        into[...] = jnp.zeros_like(into)
        for c in range(3):
            for j in range(5):
                for k in range(5):
                    first = planes[k, pl.ds(c * 32 + j, 4, stride=8)]
                    if j < 4:
                        second = planes[k, pl.ds(c * 32 + 4 + j, 4, stride=8)]
                    else:
                        second = jnp.zeros((4, LANES), f32)
                    at = c * PER + j * 40 + k * 8
                    into[at : at + 4] = jnp.where(low[:4], first, second)

    loads[0].wait()
    unpack(start_ref, held.at[0])
    for copy in loads[1:5]:
        copy.wait()
    index = lax.broadcasted_iota(jnp.int32, (64, 64), 0)
    chosen = jnp.concatenate(
        [jnp.where(index_ref[0, n : n + 1, :] == index, 1.0, 0.0) for n in range(2)], 1)
    elem_ref[...] = dot(column_ref[96:104, :64], chosen)
    elem_ref[3:4, :] = jnp.concatenate([stiff_ref[0, n : n + 1, :] for n in range(2)], 1)
    mass_w[...] = weight_ref[...] * elem_ref[3:4, :]
    weight_ref[...] = MASS_COEF * weight_ref[...]
    elem_z[cross] = elem_ref[...]
    pl.semaphore_wait(barrier, expected)

    def z_copy(source, target, sem_out, sem_in, k, back=False):
        return pltpu.make_async_remote_copy(
            src_ref=source, dst_ref=target, send_sem=sem_out.at[k - 1], recv_sem=sem_in.at[k - 1],
            device_id=z_peers[k - 1], device_id_type=MESH)

    def from_z(k):
        return lax.rem(cross + n_cross - k, n_cross)

    def reach_out(source, into, sem_out, sem_in, m):
        back = REACH.index(-REACH[m])
        return pltpu.make_async_remote_copy(
            src_ref=source, dst_ref=into.at[back], send_sem=sem_out.at[m], recv_sem=sem_in.at[back],
            device_id=(wide + REACH[m], cross), device_id_type=MESH)

    def reach_back(source, into, sem_out, sem_in, m):
        return pltpu.make_async_remote_copy(
            src_ref=source, dst_ref=into.at[m], send_sem=sem_out.at[m], recv_sem=sem_in.at[m],
            device_id=(wide + REACH[m], cross), device_id_type=MESH)

    def each_reach(make, act):
        for m, by in enumerate(REACH):
            @pl.when(within(wide, by, n_wide))
            def _(m=m):
                act(make(m))

    def sides(s, n):
        if n < 2:
            return send_x.at[s, n], got_x.at[s, n], got_x.at[s, opposite(n)]
        if n < 4:
            return send_y.at[s, n - 2], got_y.at[s, n - 2], got_y.at[s, opposite(n) - 2]
        return send_e.at[s, n - 4], got_e.at[s, n - 4], got_e.at[s, opposite(n) - 4]

    def outgoing(s, n):
        source, _, target = sides(s, n)
        return pltpu.make_async_remote_copy(
            src_ref=source, dst_ref=target, send_sem=send_sem.at[s, n],
            recv_sem=recv_sem.at[s, opposite(n)], device_id=place(n), device_id_type=MESH)

    def incoming(s, n):
        source, target, _ = sides(s, n)
        return pltpu.make_async_remote_copy(
            src_ref=source, dst_ref=target, send_sem=send_sem.at[s, n],
            recv_sem=recv_sem.at[s, n], device_id=place(n), device_id_type=MESH)

    def exchange_start(t, s):
        for n in range(4, 8):
            dx, dy = NEIGHBOURS[n]
            i, j = (4 if dx > 0 else 0), (4 if dy > 0 else 0)
            for c in range(3):
                send_e[s, n - 4, c * 8 : c * 8 + 5] = held[
                    t, pl.ds(c * PER + j * 40 + i, 5, stride=8)]
        for n in (4, 5, 6, 7):
            @pl.when(present(n))
            def _(n=n):
                outgoing(s, n).start()
        for side in range(2):
            send_x[s, side, :75] = held[t, pl.ds(4 * side, 75, stride=8)]
        for n in (0, 1):
            @pl.when(present(n))
            def _(n=n):
                outgoing(s, n).start()
        for side in range(2):
            face = jnp.concatenate(
                [held[t, c * PER + side * 160 : c * PER + side * 160 + 40] for c in range(3)], 0)
            first, second = face[:64], face[64:]
            rolled = pltpu.roll(second, 64, 1)
            use = spread_to(low if side == 0 else ~low, 56)
            send_y[s, side, :56] = jnp.where(use, first[:56], rolled)
            send_y[s, side, 56:] = first[56:]
        for n in (2, 3):
            @pl.when(present(n))
            def _(n=n):
                outgoing(s, n).start()

    def exchange_finish(t, s):
        for n in (2, 3):
            @pl.when(present(n))
            def _(n=n):
                incoming(s, n).wait_recv()
        for side in range(2):
            got = got_y[s, side]
            use = spread_to(low if side == 0 else ~low, 64)
            first = jnp.where(use, pltpu.roll(got, 64, 1), 0.0)
            second = jnp.where(use[:56], got[:56], 0.0)
            more = jnp.concatenate([first, second], 0)
            for c in range(3):
                at = c * PER + side * 160
                held[t, at : at + 40] = held[t, at : at + 40] + more[c * 40 : c * 40 + 40]
        for n in (0, 1):
            @pl.when(present(n))
            def _(n=n):
                incoming(s, n).wait_recv()
        for side in range(2):
            value = held[t, pl.ds(4 * side, 75, stride=8)] + got_x[s, side, :75]
            held[t, pl.ds(4 * side, 75, stride=8)] = value
        for n in (4, 5, 6, 7):
            @pl.when(present(n))
            def _(n=n):
                incoming(s, n).wait_recv()
        for n in range(4, 8):
            dx, dy = NEIGHBOURS[n]
            i, j = (4 if dx > 0 else 0), (4 if dy > 0 else 0)
            use = low if dy < 0 else ~low
            for c in range(3):
                more = jnp.where(use, pltpu.roll(got_e[s, n - 4, c * 8 : c * 8 + 8], 64, 1), 0.0)
                at = pl.ds(c * PER + j * 40 + i, 5, stride=8)
                held[t, at] = held[t, at] + more[:5]

    def exchange_sent(s):
        for n in range(8):
            @pl.when(present(n))
            def _(n=n):
                outgoing(s, n).wait_send()

    fibre = [elem_ref[i : i + 1, :] for i in range(3)]
    slopes = lagrange_slopes(gll_points()[0], gll_points()[0])

    def across(ref, at, table):
        total = None
        for i in range(5):
            row = jnp.broadcast_to(ref[pl.ds(at + i, 1), :], (8, LANES))
            term = column_ref[(table * 5 + i) * 8 : (table * 5 + i) * 8 + 8] * row
            total = term if total is None else total + term
        return total

    def elements(t, into):
        source = held.at[t]
        target = held.at[into]
        for c in range(3):
            for k in range(5):
                at = [c * PER + j * 40 + k * 8 for j in range(5)]
                for j, v in enumerate(along_line([source[a : a + 8] for a in at], slopes)):
                    slope_y[at[j] : at[j] + 8] = v

        def layer(j, carry):
            base = pl.multiple_of(j * 40, 8)

            def at(c, k):
                return pl.ds(pl.multiple_of(base + (c * PER + k * 8), 8), 8)

            grad_z = [along_line([source[at(c, k), :] for k in range(5)], slopes) for c in range(3)]
            flux_z = [[None] * 5 for _ in range(3)]
            for k in range(5):
                g = [
                    [across(source, base + (c * PER + k * 8), 0), slope_y[at(c, k), :], grad_z[c][k]]
                    for c in range(3)
                ]
                part = stresses(g, fibre, mass_w[at(0, k), :])
                for c in range(3):
                    flux_x[at(c, k), :] = part[c, 0]
                    flux_y[at(c, k), :] = part[c, 1]
                    flux_z[c][k] = part[c, 2]
            for c in range(3):
                pull = along_line(flux_z[c], slopes.T)
                for k in range(5):
                    mass = weight_ref[at(0, k), :] * source[at(c, k), :]
                    target[at(c, k), :] = (
                        pull[k] + mass + across(flux_x, base + (c * PER + k * 8), 1))
            return carry

        lax.fori_loop(0, 5, layer, 0)
        for c in range(3):
            for k in range(5):
                at = [c * PER + j * 40 + k * 8 for j in range(5)]
                for j, v in enumerate(along_line([flux_y[a : a + 8] for a in at], slopes.T)):
                    target[at[j] : at[j] + 8] = target[at[j] : at[j] + 8] + v

    inner = spread_to(spot > 0, 8)
    outer = spread_to(spot < 63, 8)

    def gather_local(t):
        for c in range(3):
            for j in range(5):
                at = c * PER + j * 40
                first, last = held[t, at : at + 8], held[t, at + 32 : at + 40]
                held[t, at : at + 8] = first + jnp.where(inner, pltpu.roll(last, 1, 1), 0.0)
                held[t, at + 32 : at + 40] = last + jnp.where(outer, pltpu.roll(first, 127, 1), 0.0)
            at = c * PER
            first, last = held[t, at : at + 40], held[t, at + 160 : at + 200]
            use = spread_to(low, 40)
            held[t, at : at + 40] = first + jnp.where(use, 0.0, pltpu.roll(last, 64, 1))
            held[t, at + 160 : at + 200] = spread_to(keep_y, 40) * (
                last + jnp.where(use, pltpu.roll(first, 64, 1), 0.0))
        held[t, pl.ds(4, 75, stride=8)] = held[t, pl.ds(4, 75, stride=8)] * one_x

    def square(t):
        total = jnp.zeros((8, LANES), f32)
        tail = jnp.zeros((8, LANES), f32)
        for c in range(3):
            for j in range(4):
                for k in range(5):
                    at = c * PER + j * 40 + k * 8
                    v = held[t, at : at + 8]
                    if k < 4:
                        total = total + v * v
                    else:
                        tail = tail + v * v
        total = total + jnp.where(ends, tail, 0.0)
        total = jnp.where(sub < 4, total, 0.0)
        return jnp.sum(total, axis=0, keepdims=True)

    def start_sums(slot, peers, got, order):
        for k in order:
            pltpu.make_async_remote_copy(
                src_ref=sums.at[slot, 0:1], dst_ref=got.at[k : k + 1], send_sem=sum_send.at[slot],
                recv_sem=sum_recv.at[slot], device_id=peers[k], device_id_type=MESH).start()

    def finish_sums(slot, peers, got):
        rows = got.at[0 : len(peers)]
        pltpu.make_async_copy(rows, rows, sum_recv.at[slot]).wait()
        total = sums[slot, 0:1] + jnp.sum(got[...], axis=0, keepdims=True)
        pltpu.make_async_copy(rows, rows, sum_send.at[slot]).wait()
        return total

    def in_one_row(parts):
        whole = jnp.sum(parts, axis=1, keepdims=True)
        return jnp.sum(jnp.where(lane // 32 == sub, whole, 0.0), axis=0, keepdims=True)

    def out_of_row(row):
        whole = jnp.sum(jnp.where(lane == 32 * sub, row, 0.0), axis=1, keepdims=True)
        return [jnp.broadcast_to(whole[n : n + 1], (1, LANES)) for n in range(4)]

    def greet(t):
        for stage in range(5):
            @pl.when(t == stage)
            def _(stage=stage):
                for side in range(2):
                    sign = (-1, 1)[side]
                    if stage > 0:
                        @pl.when(within(wide, sign * 2**stage, n_wide))
                        def _(side=side):
                            pl.semaphore_wait(greeting.at[stage - 1, side], 1)
                if stage < 4:
                    for side in range(2):
                        by = (-1, 1)[side] * 2 ** (stage + 1)

                        @pl.when(within(wide, by, n_wide))
                        def _(side=side, by=by):
                            pl.semaphore_signal(
                                greeting.at[stage, 1 - side], inc=1, device_id=(wide + by, cross),
                                device_id_type=MESH)

    points = gll_points()[0]
    here = jnp.where(sub < 4, 1.0, 0.0)

    def restrict(n):
        last = n == 4
        own_k = jnp.where(ends | last, 1.0, 0.0)
        own_j = jnp.where(last, keep_y, 0.0)
        own_i = here + jnp.where((sub == 4) & last, one_x, 0.0)
        columns = [column_ref[80 + 8 * i2 : 88 + 8 * i2] * own_i for i2 in range(2)]
        for c in range(3):
            lines = []
            for j in range(5):
                u = [held[n + 1, c * PER + j * 40 + k * 8 : c * PER + j * 40 + k * 8 + 8]
                     for k in range(5)]
                first, second = u[0], own_k * u[4]
                for k in range(1, 4):
                    part = float(points[k]) * u[k]
                    first, second = first + (u[k] - part), second + part
                lines.append((first, second))
            for k in range(2):
                first, second = lines[0][k], own_j * lines[4][k]
                for j in range(1, 4):
                    part = float(points[j]) * lines[j][k]
                    first, second = first + (lines[j][k] - part), second + part
                for j2, value in enumerate((first, second)):
                    for i2 in range(2):
                        row = j2 * 12 + i2 * 6 + c * 2 + k
                        rest[cross, n, row : row + 1] = jnp.sum(
                            value * columns[i2], axis=0, keepdims=True)
        for k in range(1, n_cross):
            z_copy(rest.at[cross, n], rest.at[cross, n], cz_send.at[n], cz_recv.at[n], k).start()

    def far_out(n):
        return lambda m: reach_out(
            coarse_out.at[n, 0:25], reach_in.at[n], cr_send.at[n], cr_recv.at[n], m)

    def far_back(n):
        return lambda m: reach_back(
            coarse_out.at[n, 0:25], reach_in.at[n], cr_send.at[n], cr_recv.at[n], m)

    def hand_on(n):
        for k in range(1, n_cross):
            z_copy(
                rest.at[from_z(k), n], rest.at[from_z(k), n], cz_send.at[n], cz_recv.at[n], k
            ).wait_recv()
        before = jnp.zeros((12, LANES), f32)
        for q in range(4):
            ahead = rest[q, n, 12:24]
            swapped = pltpu.roll(jnp.where(spread_to(low, 12), ahead, before), 64, 1)
            before = ahead
            value = rest[q, n, 0:12] + swapped
            moved = pltpu.roll(value, 1, 1)
            for i2 in range(2):
                for c in range(3):
                    first, last = i2 * 6 + c * 2, i2 * 6 + c * 2 + 1
                    row = i2 * 12 + q * 3 + c
                    coarse_out[n, row : row + 1] = value[first : first + 1] + jnp.where(
                        inner[:1], moved[last : last + 1], 0.0)
                    tails[row : row + 1] = value[last : last + 1]
        late = pltpu.roll(
            jnp.where(spread_to(ends, 24), tails[...], 0.0), 1, 1, stride=1, stride_axis=0)
        coarse_out[n, 24:25] = jnp.sum(late, axis=0, keepdims=True)
        each_reach(far_out(n), lambda c: c.start())
        for k in range(1, n_cross):
            z_copy(
                rest.at[cross, n], rest.at[cross, n], cz_send.at[n], cz_recv.at[n], k).wait_send()

    def elements_out():
        for k in range(1, n_cross):
            z_copy(elem_z.at[cross], elem_z.at[cross], ez_send, ez_recv, k).start()

    def elements_on():
        for k in range(1, n_cross):
            z_copy(elem_z.at[from_z(k)], elem_z.at[from_z(k)], ez_send, ez_recv, k).wait_recv()
        for q in range(4):
            for m in range(4):
                elem_out[m * 4 + q : m * 4 + q + 1] = elem_z[q, m : m + 1]
        each_reach(
            lambda m: reach_out(elem_out, elem_in, er_send, er_recv, m), lambda c: c.start())
        for k in range(1, n_cross):
            z_copy(elem_z.at[cross], elem_z.at[cross], ez_send, ez_recv, k).wait_send()

    def apply_all(base, squares, late=None):
        def step(t, carry):
            elements(t, t + 1)
            gather_local(t + 1)

            @pl.when(t == 0)
            def _():
                held[1] = load[...] - held[1]

            s = lax.rem(t + base, 2)
            exchange_start(t + 1, s)
            exchange_sent(1 - s)
            if squares:
                greet(t)
                norms[pl.ds(t, 1)] = square(t)

                @pl.when(t >= 1)
                def _():
                    restrict(t - 1)

                @pl.when(t == 1)
                def _():
                    elements_out()

                @pl.when(t >= 2)
                def _():
                    hand_on(t - 2)

                @pl.when(t == 3)
                def _():
                    elements_on()
            if late is not None:
                @pl.when(t == 3)
                def _():
                    late()
            exchange_finish(t + 1, s)
            return carry

        lax.fori_loop(0, 4, step, 0)

    exchange_start(0, 0)
    loads[5].wait()
    unpack(rhs_ref, load)
    exchange_finish(0, 0)
    apply_all(1, True)
    norms[4:5] = square(4)
    sums[0, 0:1] = in_one_row(norms[1:9])
    start_sums(0, z_peers, got_z, range(3))
    elements(4, 5)
    restrict(4)
    greet(4)
    restrict(3)
    hand_on(2)
    sums[1, 0:1] = finish_sums(0, z_peers, got_z)
    start_sums(1, w_peers, got_w.at[0], FAR_FIRST)
    hand_on(4)
    hand_on(3)

    each_reach(lambda m: reach_back(elem_out, elem_in, er_send, er_recv, m), lambda c: c.wait_recv())
    for m, by in enumerate(REACH):
        if by >= -HOME:
            elem_c[pl.ds(HOME + by, 16, stride=8)] = elem_in[m]
    elem_c[pl.ds(HOME, 16, stride=8)] = elem_out[...]
    for q in range(4):
        at = (12 + q) * 8
        elem_c[at : at + 8] = jnp.where(sub < 7, elem_c[at : at + 8], 0.0)
    each_reach(lambda m: reach_out(elem_out, elem_in, er_send, er_recv, m), lambda c: c.wait_send())

    for n in (0, 1, 2, 3, 4):
        each_reach(far_back(n), lambda c: c.wait_recv())
    largest = estimate(out_of_row(finish_sums(1, w_peers, got_w.at[0])))
    step_poly, rest_poly = smoothing(largest, FINE_RATIO)

    free = jnp.where(wide - HOME + sub < n_wide, 1.0, 0.0)
    for by in (0,) + REACH:
        part = None
        for n in range(5):
            source = coarse_out.at[n] if by == 0 else reach_in.at[n, REACH.index(by)]
            term = rest_poly[n] * source[0:25]
            part = term if part is None else part + term
        for i2 in range(2):
            s = HOME + by + i2
            if 0 <= s < 8:
                gather[pl.ds(i2 * 96 + s, 12, stride=8)] = part[i2 * 12 : i2 * 12 + 12]
                tail_in[i2 * 8 + s : i2 * 8 + s + 1] = part[24:25]
    for m in range(12):
        first = gather[m * 8 : m * 8 + 8] + gather[96 + m * 8 : 104 + m * 8]
        last = pltpu.roll(tail_in[0:8], 127 - m, 1) + pltpu.roll(tail_in[8:16], 115 - m, 1)
        vertex[0, m * 16 : m * 16 + 8] = first * free
        vertex[0, m * 16 + 8 : m * 16 + 16] = free * jnp.where(
            outer, pltpu.roll(first, 127, 1), last)

    def close(n, q):
        for c in range(3):
            at = (q * 6 + c * 2) * 8
            first, last = gather[pl.ds(at, 8)], gather[pl.ds(at + 8, 8)]
            first = first + jnp.where(inner, pltpu.roll(last, 1, 1), 0.0)
            vertex[n, pl.ds(at, 8)] = first * free
            vertex[n, pl.ds(at + 8, 8)] = free * jnp.where(outer, pltpu.roll(first, 127, 1), last)

    def close_all(n):
        for q in range(4):
            close(n, q)

    def coarse_step(n, carry):
        carried = {}

        def column(q):
            def at(c, k, up=0):
                return pl.ds((q + up) * 48 + c * 16 + k * 8, 8)

            def data(m):
                return elem_c[m * 32 + q * 8 : m * 32 + q * 8 + 8]

            fib = [data(0), data(1), data(2)]
            stiff = data(3)
            mass = jnp.where(stiff > 0.0, MASS_COEF, 0.0)
            modes = []
            for c in range(3):
                m = {}
                for k in range(2):
                    w = vertex[n, at(c, k), :]
                    beside = pltpu.roll(jnp.where(low, vertex[n, at(c, k, 1), :], w), 64, 1)
                    for b, v in enumerate((w + beside, beside - w)):
                        after = pltpu.roll(v, 7, 0)
                        m[0, b, k], m[1, b, k] = v + after, after - v
                modes.append({})
                for a in range(2):
                    for b in range(2):
                        first, last = m[a, b, 0], m[a, b, 1]
                        modes[c][a, b, 0], modes[c][a, b, 1] = first + last, last - first
            back = [{}, {}, {}]

            def put(c, mode, value):
                back[c][mode] = back[c][mode] + value if mode in back[c] else value

            for ones, weight in (((0, 0, 0), 16.0), ((1, 0, 0), 48.0), ((0, 1, 0), 48.0), ((0, 0, 1), 48.0)):
                at_mode = {
                    d: tuple(1 if d == e else ones[e] for e in range(3))
                    for d in range(3) if not ones[d]
                }
                grad = [
                    [modes[c][at_mode[d]] if d in at_mode else None for d in range(3)]
                    for c in range(3)
                ]
                part = stresses(grad, fib, stiff * (1.0 / weight))
                for d in at_mode:
                    for c in range(3):
                        put(c, at_mode[d], part[c, d])
            top = [modes[c][1, 1, 1] for c in range(3)]
            along = fib[0] * top[0] + fib[1] * top[1] + fib[2] * top[2]
            along = (stiff * (TOP_ALONG / 144.0)) * along
            top_scale = stiff * (TOP_SELF / 144.0)
            for c in range(3):
                put(c, (1, 1, 1), top_scale * top[c] + along * fib[c])
                for mode, value in modes[c].items():
                    count = sum(mode)
                    put(c, mode, (mass * (0.25 ** (3 - count) / 12.0**count)) * value)
                for k in range(2):
                    w = []
                    xs = {}
                    for a in range(2):
                        for b in range(2):
                            first, last = back[c][a, b, 0], back[c][a, b, 1]
                            xs[a, b] = first + last if k else first - last
                    for b in range(2):
                        w.append((xs[0, b] - xs[1, b]) + pltpu.roll(xs[0, b] + xs[1, b], 1, 0))
                    other = pltpu.roll(w[0] + w[1], 64, 1)
                    own = jnp.where(low, carried[c, k], other) if q else jnp.where(low, 0.0, other)
                    gather[at(c, k), :] = (w[0] - w[1]) + own
                    carried[c, k] = other

        for q in range(4):
            column(q)
        close_all(n + 1)
        return carry

    lax.fori_loop(0, 3, coarse_step, 0)

    def coarse_square(n):
        total = jnp.zeros((8, LANES), f32)
        tail = jnp.zeros((8, LANES), f32)
        for m in range(12):
            first, last = vertex[n, m * 16 : m * 16 + 8], vertex[n, m * 16 + 8 : m * 16 + 16]
            total = total + first * first
            tail = tail + last * last
        return (total + jnp.where(ends, tail, 0.0))[HOME : HOME + 1]

    for n in range(4):
        norms[n : n + 1] = coarse_square(n)
    sums[2, 0:1] = in_one_row(norms[0:8])
    start_sums(2, w_peers, got_w.at[1], FAR_FIRST)
    for n in range(5):
        each_reach(far_out(n), lambda c: c.wait_send())
    def add_steps(c, carry):
        at = pl.ds(pl.multiple_of(c * PER, 8), PER)
        value = held[0, at]
        for n in range(4):
            value = value + step_poly[n] * held[n + 1, at]
        held[0, at] = value
        return carry

    lax.fori_loop(0, 3, add_steps, 0)
    coarse_largest = estimate(out_of_row(finish_sums(2, w_peers, got_w.at[1])))
    coarse_poly, _ = smoothing(coarse_largest, COARSE_RATIO)
    left, right = column_ref[80:88], column_ref[88:96]
    for c in range(3):
        ends_k = []
        for k in range(2):
            w = []
            for up in range(2):
                at = pl.ds(pl.multiple_of((cross + up) * 48, 8) + (c * 16 + k * 8), 8)
                value = coarse_poly[0] * vertex[0, at]
                for n in range(1, 4):
                    value = value + coarse_poly[n] * vertex[n, at]
                w.append(value)
            ends_k.append((w[0], pltpu.roll(jnp.where(low, w[1], w[0]), 64, 1)))
        own = [ends_k[k][0][HOME : HOME + 1] for k in range(2)]
        for ey in range(2):
            a, b = own if ey == 0 else [pltpu.roll(v, 64, 1) for v in own]
            line = jnp.where(low[:1], a, pltpu.roll(b, 1, 1))
            cor_ref[c, 0, ey : ey + 1, :] = line[:, :65]
        nodes = []
        for k in range(2):
            first, last = [
                left * jnp.broadcast_to(v[HOME : HOME + 1], (8, LANES))
                + right * jnp.broadcast_to(v[HOME + 1 : HOME + 2], (8, LANES))
                for v in ends_k[k]
            ]
            step = last - first
            nodes.append(
                [first] + [first + float(points[j]) * step for j in range(1, 4)] + [last])
        for j in range(5):
            first, last = nodes[0][j], nodes[1][j]
            step = last - first
            for k in range(5):
                at = c * PER + j * 40 + k * 8
                more = first if k == 0 else last if k == 4 else first + float(points[k]) * step
                held[0, at : at + 8] = held[0, at : at + 8] + more

    row = lax.broadcasted_iota(jnp.int32, (256, 256), 0)
    z_at = lax.broadcasted_iota(jnp.int32, (256, 256), 1)
    spread = jnp.where(z_at == 4 * lax.rem(row, 64) + row // 64, 1.0, 0.0).astype(jnp.bfloat16)

    def to_nodes(value_at, ref):
        for c in range(3):
            for j in range(4):
                for k in range(5):
                    value = value_at(pl.ds(c * PER + j * 40 + k * 8, 8))
                    planes[k, pl.ds(c * 32 + j, 4, stride=8)] = value[:4]
                    planes[k, pl.ds(c * 32 + 4 + j, 4, stride=8)] = pltpu.roll(value, 64, 1)[:4]
        use = spread_to(low, 96)
        joined = jnp.concatenate(
            [jnp.where(use, planes[k], pltpu.roll(planes[k + 1], 64, 1)) for k in (0, 2)], 1)
        ref[:, :, :, 0:256] = selected(joined, spread).reshape(3, 4, 8, 256)
        ref[:, :, :, 256:257] = planes[4][:, 63:64].reshape(3, 4, 8, 1)

    def most(at):
        value = held[0, at]
        for n in range(3):
            value = value + step_poly[n] * held[n + 1, at]
        return value

    apply_all(1, False, lambda: to_nodes(most, out_ref))
    to_nodes(lambda at: step_poly[3] * held[4, at], last_ref)
    exchange_sent(0)


def on_device(rhs, start, stiffness, fibre_index):
    operands = [start, rhs, stiffness, fibre_index] + tables()
    vmem = pl.BlockSpec(memory_space=pltpu.VMEM)
    f32 = jnp.float32

    def room(*shape):
        return pltpu.VMEM(shape, f32)

    def flags(*shape):
        return pltpu.SemaphoreType.DMA(shape)

    most, last, correction = pl.pallas_call(
        kernel,
        out_shape=(
            jax.ShapeDtypeStruct(rhs.shape, f32),
            jax.ShapeDtypeStruct(rhs.shape, f32),
            jax.ShapeDtypeStruct((3, 1, 2, 65), f32),
        ),
        in_specs=[pl.BlockSpec(memory_space=pltpu.HBM)] * len(operands),
        out_specs=(vmem, vmem, vmem),
        scratch_shapes=[
            room(3, 4, 8, 257),
            room(3, 4, 8, 257),
            room(1, 2, 64),
            pltpu.VMEM((1, 2, 64), jnp.int32),
            room(PER, LANES),
            room(104, LANES),
            room(8, LANES),
            room(6, ROWS, LANES),
            room(ROWS, LANES),
            room(PER, LANES),
            room(ROWS, LANES),
            room(ROWS, LANES),
            room(ROWS, LANES),
            room(5, 96, LANES),
            room(2, 2, FACE_X, LANES),
            room(2, 2, FACE_Y, LANES),
            room(2, 4, EDGE, LANES),
            room(2, 2, FACE_X, LANES),
            room(2, 2, FACE_Y, LANES),
            room(2, 4, EDGE, LANES),
            room(4, 5, 24, LANES),
            room(5, 32, LANES),
            room(24, LANES),
            room(16, LANES),
            room(5, 8, 25, LANES),
            room(4, 8, LANES),
            room(16, LANES),
            room(8, 16, LANES),
            room(128, LANES),
            room(4, 240, LANES),
            room(240, LANES),
            room(3, 8, LANES),
            room(16, LANES),
            room(8, LANES),
            room(2, 32, LANES),
            flags(2, 8), flags(2, 8),
            flags(3), flags(3),
            flags(3), flags(3),
            flags(5, 3), flags(5, 3),
            flags(8), flags(8),
            flags(5, 8), flags(5, 8),
            flags(6),
            pltpu.SemaphoreType.REGULAR((4, 2)),
        ],
        compiler_params=pltpu.CompilerParams(
            collective_id=0, has_side_effects=True, vmem_limit_bytes=60 * 1024 * 1024
        ),
    )(*operands)
    return most + last, correction


def solution(mesh):
    in_specs = (
        P(None, "wide", "cross", None),
        P(None, "wide", "cross", None),
        P("wide", "cross", None),
        P("wide", "cross", None),
    )
    out_specs = (P(None, "wide", "cross", None), P(None, "wide", "cross", None))
    return jax.shard_map(
        on_device, mesh=mesh, in_specs=in_specs, out_specs=out_specs, check_vma=False
    )
```

```python
import functools
import math

import jax
import jax.numpy as jnp
import numpy as np
from jax import lax
from jax.experimental import pallas as pl
from jax.experimental.pallas import tpu as pltpu
from jax.sharding import PartitionSpec as P

NFIB = 64
LAMBDA_COEF = 2.0
SHEAR_CROSS = 1.0
SHEAR_ALONG = 3.0
FIBRE_COEF = 20.0
MASS_COEF = 0.02
FINE_RATIO = 10.0
COARSE_RATIO = 30.0

MESH = pl.DeviceIdType.MESH
LANES = 128
PER = 200
ROWS = 3 * PER
NEIGHBOURS = ((-1, 0), (1, 0), (0, -1), (0, 1), (-1, -1), (-1, 1), (1, -1), (1, 1))
FACE_X, FACE_Y, EDGE = 80, 64, 24
REACH = (-4, -3, -2, -1, 1, 2, 3, 4)
HOME = 3
FAR_FIRST = sorted(range(31), key=lambda k: -min(k + 1, 31 - k))
TOP_SELF = LAMBDA_COEF + 4.0 * SHEAR_CROSS + (SHEAR_ALONG - SHEAR_CROSS)
TOP_ALONG = 5.0 * (SHEAR_ALONG - SHEAR_CROSS) + FIBRE_COEF


def gll_points():
    root = math.sqrt(3.0 / 7.0)
    points = (np.array([-1.0, -root, 0.0, root, 1.0]) + 1.0) / 2.0
    weights = np.array([0.1, 49.0 / 90.0, 32.0 / 45.0, 49.0 / 90.0, 0.1]) / 2.0
    return (points, weights)


def lagrange_slopes(points, where):
    count = len(points)
    table = np.zeros((len(where), count))
    for i, spot in enumerate(where):
        for j in range(count):
            total = 0.0
            for k in range(count):
                if k == j:
                    continue
                term = 1.0 / (points[j] - points[k])
                for m in range(count):
                    if m != j and m != k:
                        term = term * (spot - points[m]) / (points[j] - points[m])
                total = total + term
            table[i, j] = total
    return table


def tables():
    points, weights = gll_points()
    slopes = lagrange_slopes(points, points)
    cube = np.zeros((5, 5, 8))
    cube[..., :5] = weights[:, None, None] * weights[None, :, None] * weights[None, None, :]
    columns = np.zeros((12, 8, LANES))
    columns[0:5, :5] = slopes.T[:, :, None]
    columns[5:10, :5] = slopes[:, :, None]
    columns[10, :5] = (1.0 - points)[:, None]
    columns[11, :5] = points[:, None]
    columns = columns.reshape(96, LANES)
    angle = np.arange(NFIB) * (2.0 * math.pi / NFIB)
    tilt = 0.4 * np.sin(3.0 * angle)
    fibre = np.zeros((8, LANES))
    fibre[:3, :NFIB] = [np.cos(angle) * np.cos(tilt), np.sin(angle) * np.cos(tilt), np.sin(tilt)]
    parts = (
        np.broadcast_to(cube.reshape(-1)[:, None], (PER, LANES)),
        np.concatenate([columns, fibre], 0),
    )
    return [jnp.asarray(np.ascontiguousarray(part), dtype=jnp.float32) for part in parts]


def dot(a, b):
    return jnp.dot(
        a, b, precision=lax.Precision.HIGHEST, preferred_element_type=jnp.float32
    )


def selected(values, pick):
    rows = values.shape[0]
    high = values.astype(jnp.bfloat16)
    left = values - high.astype(jnp.float32)
    middle = left.astype(jnp.bfloat16)
    low = (left - middle.astype(jnp.float32)).astype(jnp.bfloat16)
    out = jnp.dot(
        jnp.concatenate([high, middle, low], 0), pick, preferred_element_type=jnp.float32)
    return (out[:rows] + out[rows : 2 * rows]) + out[2 * rows :]


def along_line(u, table):
    half = lambda i, j: 0.5 * (float(table[i, j]) + float(table[i, 4 - j]))
    odd_half = lambda i, j: 0.5 * (float(table[i, j]) - float(table[i, 4 - j]))
    even = [u[0] + u[4], u[1] + u[3]]
    odd = [u[0] - u[4], u[1] - u[3]]
    p = [
        half(i, 0) * even[0] + half(i, 1) * even[1] + float(table[i, 2]) * u[2] for i in range(2)
    ]
    q = [odd_half(i, 0) * odd[0] + odd_half(i, 1) * odd[1] for i in range(3)]
    return [q[0] + p[0], q[1] + p[1], q[2], q[1] - p[1], q[0] - p[0]]


def plus(*terms):
    total = None
    for term in terms:
        if term is not None:
            total = term if total is None else total + term
    return total


def times(a, b):
    return None if a is None or b is None else a * b


def stresses(grad, fibre, scale):
    twice = {}
    for i in range(3):
        for j in range(i, 3):
            twice[i, j] = twice[j, i] = (
                times(grad[i][i], 2.0) if i == j else plus(grad[i][j], grad[j][i]))
    trace = times(plus(grad[0][0], grad[1][1], grad[2][2]), LAMBDA_COEF)
    along = [plus(*[times(twice[i, j], fibre[j]) for j in range(3)]) for i in range(3)]
    stretch = plus(*[times(along[i], fibre[i]) for i in range(3)])
    half = (0.25 * FIBRE_COEF) * stretch
    cross = SHEAR_ALONG - SHEAR_CROSS
    pull = [cross * along[i] + half * fibre[i] for i in range(3)]
    out = {}
    for i in range(3):
        for j in range(i, 3):
            value = plus(
                times(twice[i, j], SHEAR_CROSS) if SHEAR_CROSS != 1.0 else twice[i, j],
                fibre[i] * pull[j] + pull[i] * fibre[j] if i != j else (2.0 * fibre[i]) * pull[i],
                trace if i == j else None)
            out[i, j] = out[j, i] = value * scale
    return out


def estimate(n):
    scale = 1.0 / (n[0] + 1e-6)
    for k in range(1, 3):
        scale = scale / (n[k] * scale + 1e-6)
    return jnp.sqrt(n[3] * scale + 1e-6)


def smoothing(largest, ratio):
    upper = 1.1
    lower = upper / ratio
    centre, radius = 0.5 * (upper + lower), 0.5 * (upper - lower)
    spread = centre / radius
    weight = 1.0 / spread
    step = np.array([1.0 / centre, 0.0, 0.0, 0.0, 0.0])
    rest = np.array([1.0, 0.0, 0.0, 0.0, 0.0])
    total = np.zeros(5)
    for k in range(4):
        total = total + step
        rest = rest - np.concatenate([[0.0], step[:4]])
        if k < 3:
            new = 1.0 / (2.0 * spread - weight)
            step = new * weight * step + 2.0 * new / radius * rest
            weight = new
    inverse = 1.0 / largest
    powers = [None, inverse]
    for n in range(2, 5):
        powers.append(powers[-1] * inverse)
    rests = [float(rest[n]) * (powers[n] if n else jnp.ones_like(largest)) for n in range(5)]
    return [float(total[n]) * powers[n + 1] for n in range(4)], rests


def kernel(
    start_hbm, rhs_hbm, stiff_hbm, index_hbm, weight_hbm, column_hbm,
    out_ref, last_ref, cor_ref,
    start_ref, rhs_ref, stiff_ref, index_ref, weight_ref, column_ref, elem_ref,
    held, load, mass_w, slope_y, flux_x, flux_y, planes,
    send_x, send_y, send_e, got_x, got_y, got_e,
    rest, coarse_out, tails, tail_in, reach_in, elem_z, elem_out, elem_in, elem_c, vertex, gather,
    sums, norms, got_z, got_w,
    send_sem, recv_sem, sum_send, sum_recv, ez_send, ez_recv, cz_send, cz_recv,
    er_send, er_recv, cr_send, cr_recv, in_sem, greeting,
):
    wide, cross = lax.axis_index("wide"), lax.axis_index("cross")
    n_wide, n_cross = lax.axis_size("wide"), lax.axis_size("cross")
    f32 = jnp.float32

    def within(at, by, size):
        return at >= -by if by < 0 else at < size - by

    def present(n):
        dx, dy = NEIGHBOURS[n]
        inside = None
        for here, by, size in ((wide, dx, n_wide), (cross, dy, n_cross)):
            if by:
                ok = within(here, by, size)
                inside = ok if inside is None else inside & ok
        return inside

    def place(n):
        dx, dy = NEIGHBOURS[n]
        return (wide + dx, cross + dy)

    def opposite(n):
        dx, dy = NEIGHBOURS[n]
        return NEIGHBOURS.index((-dx, -dy))

    z_peers = [(wide, lax.rem(cross + k, n_cross)) for k in range(1, n_cross)]
    w_peers = [(lax.rem(wide + k, n_wide), cross) for k in range(1, n_wide)]

    loads = [
        pltpu.make_async_copy(source, target, in_sem.at[n])
        for n, (source, target) in enumerate((
            (start_hbm, start_ref), (stiff_hbm, stiff_ref), (index_hbm, index_ref),
            (column_hbm, column_ref), (weight_hbm, weight_ref), (rhs_hbm, rhs_ref)))
    ]
    for copy in loads:
        copy.start()

    got_x[...] = jnp.zeros_like(got_x)
    got_y[...] = jnp.zeros_like(got_y)
    got_e[...] = jnp.zeros_like(got_e)
    reach_in[...] = jnp.zeros_like(reach_in)
    elem_in[...] = jnp.zeros_like(elem_in)
    got_z[...] = jnp.zeros_like(got_z)
    got_w[...] = jnp.zeros_like(got_w)
    barrier = pltpu.get_barrier_semaphore()
    expected = jnp.int32(0)
    for n in (4, 5, 6, 7, 0, 1, 2, 3):
        @pl.when(present(n))
        def _(n=n):
            pl.semaphore_signal(barrier, inc=1, device_id=place(n), device_id_type=MESH)
        expected = expected + present(n).astype(jnp.int32)

    lane = lax.broadcasted_iota(jnp.int32, (8, LANES), 1)
    sub = lax.broadcasted_iota(jnp.int32, (8, LANES), 0)
    spot = lax.rem(lane, 64)
    low = lane < 64
    ends = spot == 63
    one_x = jnp.where(wide < n_wide - 1, 1.0, 0.0)
    one_y = jnp.where(cross < n_cross - 1, 1.0, 0.0)
    keep_y = jnp.where(low, 1.0, one_y)

    def spread_to(mask, rows):
        return jnp.broadcast_to(mask[:1], (rows, LANES))

    send_x[...] = jnp.zeros_like(send_x)
    send_e[...] = jnp.zeros_like(send_e)
    sums[...] = jnp.zeros_like(sums)
    norms[...] = jnp.zeros_like(norms)
    vertex[...] = jnp.zeros_like(vertex)
    gather[...] = jnp.zeros_like(gather)
    tail_in[...] = jnp.zeros_like(tail_in)
    coarse_out[...] = jnp.zeros_like(coarse_out)
    z_at = lax.broadcasted_iota(jnp.int32, (256, 5 * LANES), 0)
    col = lax.broadcasted_iota(jnp.int32, (256, 5 * LANES), 1)
    pick = jnp.where(z_at == 4 * lax.rem(col, 64) + col // LANES, 1.0, 0.0).astype(jnp.bfloat16)

    def unpack(ref, into):
        nodes = selected(ref[:, :, :, 0:256].reshape(96, 256), pick)
        final = jnp.broadcast_to(ref[:, :, :, 256:257].reshape(96, 1), (96, LANES))
        for k in range(5):
            part = nodes[:, k * LANES : k * LANES + LANES]
            planes[k] = jnp.where(spread_to(ends, 96), final, part) if k == 4 else part
        into[...] = jnp.zeros_like(into)
        for c in range(3):
            for j in range(5):
                for k in range(5):
                    first = planes[k, pl.ds(c * 32 + j, 4, stride=8)]
                    if j < 4:
                        second = planes[k, pl.ds(c * 32 + 4 + j, 4, stride=8)]
                    else:
                        second = jnp.zeros((4, LANES), f32)
                    at = c * PER + j * 40 + k * 8
                    into[at : at + 4] = jnp.where(low[:4], first, second)

    loads[0].wait()
    unpack(start_ref, held.at[0])
    for copy in loads[1:5]:
        copy.wait()
    index = lax.broadcasted_iota(jnp.int32, (64, 64), 0)
    chosen = jnp.concatenate(
        [jnp.where(index_ref[0, n : n + 1, :] == index, 1.0, 0.0) for n in range(2)], 1)
    elem_ref[...] = dot(column_ref[96:104, :64], chosen)
    elem_ref[3:4, :] = jnp.concatenate([stiff_ref[0, n : n + 1, :] for n in range(2)], 1)
    mass_w[...] = weight_ref[...] * elem_ref[3:4, :]
    weight_ref[...] = MASS_COEF * weight_ref[...]
    elem_z[cross] = elem_ref[...]
    pl.semaphore_wait(barrier, expected)

    def z_copy(source, target, sem_out, sem_in, k, back=False):
        return pltpu.make_async_remote_copy(
            src_ref=source, dst_ref=target, send_sem=sem_out.at[k - 1], recv_sem=sem_in.at[k - 1],
            device_id=z_peers[k - 1], device_id_type=MESH)

    def from_z(k):
        return lax.rem(cross + n_cross - k, n_cross)

    def reach_out(source, into, sem_out, sem_in, m):
        back = REACH.index(-REACH[m])
        return pltpu.make_async_remote_copy(
            src_ref=source, dst_ref=into.at[back], send_sem=sem_out.at[m], recv_sem=sem_in.at[back],
            device_id=(wide + REACH[m], cross), device_id_type=MESH)

    def reach_back(source, into, sem_out, sem_in, m):
        return pltpu.make_async_remote_copy(
            src_ref=source, dst_ref=into.at[m], send_sem=sem_out.at[m], recv_sem=sem_in.at[m],
            device_id=(wide + REACH[m], cross), device_id_type=MESH)

    def each_reach(make, act):
        for m, by in enumerate(REACH):
            @pl.when(within(wide, by, n_wide))
            def _(m=m):
                act(make(m))

    def sides(s, n):
        if n < 2:
            return send_x.at[s, n], got_x.at[s, n], got_x.at[s, opposite(n)]
        if n < 4:
            return send_y.at[s, n - 2], got_y.at[s, n - 2], got_y.at[s, opposite(n) - 2]
        return send_e.at[s, n - 4], got_e.at[s, n - 4], got_e.at[s, opposite(n) - 4]

    def outgoing(s, n):
        source, _, target = sides(s, n)
        return pltpu.make_async_remote_copy(
            src_ref=source, dst_ref=target, send_sem=send_sem.at[s, n],
            recv_sem=recv_sem.at[s, opposite(n)], device_id=place(n), device_id_type=MESH)

    def incoming(s, n):
        source, target, _ = sides(s, n)
        return pltpu.make_async_remote_copy(
            src_ref=source, dst_ref=target, send_sem=send_sem.at[s, n],
            recv_sem=recv_sem.at[s, n], device_id=place(n), device_id_type=MESH)

    def exchange_start(t, s):
        for n in range(4, 8):
            dx, dy = NEIGHBOURS[n]
            i, j = (4 if dx > 0 else 0), (4 if dy > 0 else 0)
            for c in range(3):
                send_e[s, n - 4, c * 8 : c * 8 + 5] = held[
                    t, pl.ds(c * PER + j * 40 + i, 5, stride=8)]
        for n in (4, 5, 6, 7):
            @pl.when(present(n))
            def _(n=n):
                outgoing(s, n).start()
        for side in range(2):
            send_x[s, side, :75] = held[t, pl.ds(4 * side, 75, stride=8)]
        for n in (0, 1):
            @pl.when(present(n))
            def _(n=n):
                outgoing(s, n).start()
        for side in range(2):
            face = jnp.concatenate(
                [held[t, c * PER + side * 160 : c * PER + side * 160 + 40] for c in range(3)], 0)
            first, second = face[:64], face[64:]
            rolled = pltpu.roll(second, 64, 1)
            use = spread_to(low if side == 0 else ~low, 56)
            send_y[s, side, :56] = jnp.where(use, first[:56], rolled)
            send_y[s, side, 56:] = first[56:]
        for n in (2, 3):
            @pl.when(present(n))
            def _(n=n):
                outgoing(s, n).start()

    def exchange_finish(t, s):
        for n in (2, 3):
            @pl.when(present(n))
            def _(n=n):
                incoming(s, n).wait_recv()
        for side in range(2):
            got = got_y[s, side]
            use = spread_to(low if side == 0 else ~low, 64)
            first = jnp.where(use, pltpu.roll(got, 64, 1), 0.0)
            second = jnp.where(use[:56], got[:56], 0.0)
            more = jnp.concatenate([first, second], 0)
            for c in range(3):
                at = c * PER + side * 160
                held[t, at : at + 40] = held[t, at : at + 40] + more[c * 40 : c * 40 + 40]
        for n in (0, 1):
            @pl.when(present(n))
            def _(n=n):
                incoming(s, n).wait_recv()
        for side in range(2):
            value = held[t, pl.ds(4 * side, 75, stride=8)] + got_x[s, side, :75]
            held[t, pl.ds(4 * side, 75, stride=8)] = value
        for n in (4, 5, 6, 7):
            @pl.when(present(n))
            def _(n=n):
                incoming(s, n).wait_recv()
        for n in range(4, 8):
            dx, dy = NEIGHBOURS[n]
            i, j = (4 if dx > 0 else 0), (4 if dy > 0 else 0)
            use = low if dy < 0 else ~low
            for c in range(3):
                more = jnp.where(use, pltpu.roll(got_e[s, n - 4, c * 8 : c * 8 + 8], 64, 1), 0.0)
                at = pl.ds(c * PER + j * 40 + i, 5, stride=8)
                held[t, at] = held[t, at] + more[:5]

    def exchange_sent(s):
        for n in range(8):
            @pl.when(present(n))
            def _(n=n):
                outgoing(s, n).wait_send()

    fibre = [elem_ref[i : i + 1, :] for i in range(3)]
    slopes = lagrange_slopes(gll_points()[0], gll_points()[0])

    def across(ref, at, table):
        total = None
        for i in range(5):
            row = jnp.broadcast_to(ref[pl.ds(at + i, 1), :], (8, LANES))
            term = column_ref[(table * 5 + i) * 8 : (table * 5 + i) * 8 + 8] * row
            total = term if total is None else total + term
        return total

    def elements(t, into):
        source = held.at[t]
        target = held.at[into]
        for c in range(3):
            for k in range(5):
                at = [c * PER + j * 40 + k * 8 for j in range(5)]
                for j, v in enumerate(along_line([source[a : a + 8] for a in at], slopes)):
                    slope_y[at[j] : at[j] + 8] = v

        def layer(j, carry):
            base = pl.multiple_of(j * 40, 8)

            def at(c, k):
                return pl.ds(pl.multiple_of(base + (c * PER + k * 8), 8), 8)

            grad_z = [along_line([source[at(c, k), :] for k in range(5)], slopes) for c in range(3)]
            flux_z = [[None] * 5 for _ in range(3)]
            for k in range(5):
                g = [
                    [across(source, base + (c * PER + k * 8), 0), slope_y[at(c, k), :], grad_z[c][k]]
                    for c in range(3)
                ]
                part = stresses(g, fibre, mass_w[at(0, k), :])
                for c in range(3):
                    flux_x[at(c, k), :] = part[c, 0]
                    flux_y[at(c, k), :] = part[c, 1]
                    flux_z[c][k] = part[c, 2]
            for c in range(3):
                pull = along_line(flux_z[c], slopes.T)
                for k in range(5):
                    mass = weight_ref[at(0, k), :] * source[at(c, k), :]
                    target[at(c, k), :] = (
                        pull[k] + mass + across(flux_x, base + (c * PER + k * 8), 1))
            return carry

        lax.fori_loop(0, 5, layer, 0, unroll=True)
        for c in range(3):
            for k in range(5):
                at = [c * PER + j * 40 + k * 8 for j in range(5)]
                for j, v in enumerate(along_line([flux_y[a : a + 8] for a in at], slopes.T)):
                    target[at[j] : at[j] + 8] = target[at[j] : at[j] + 8] + v

    inner = spread_to(spot > 0, 8)
    outer = spread_to(spot < 63, 8)

    def gather_local(t):
        for c in range(3):
            for j in range(5):
                at = c * PER + j * 40
                first, last = held[t, at : at + 8], held[t, at + 32 : at + 40]
                held[t, at : at + 8] = first + jnp.where(inner, pltpu.roll(last, 1, 1), 0.0)
                held[t, at + 32 : at + 40] = last + jnp.where(outer, pltpu.roll(first, 127, 1), 0.0)
            at = c * PER
            first, last = held[t, at : at + 40], held[t, at + 160 : at + 200]
            use = spread_to(low, 40)
            held[t, at : at + 40] = first + jnp.where(use, 0.0, pltpu.roll(last, 64, 1))
            held[t, at + 160 : at + 200] = spread_to(keep_y, 40) * (
                last + jnp.where(use, pltpu.roll(first, 64, 1), 0.0))
        held[t, pl.ds(4, 75, stride=8)] = held[t, pl.ds(4, 75, stride=8)] * one_x

    def square(t):
        total = jnp.zeros((8, LANES), f32)
        tail = jnp.zeros((8, LANES), f32)
        for c in range(3):
            for j in range(4):
                for k in range(5):
                    at = c * PER + j * 40 + k * 8
                    v = held[t, at : at + 8]
                    if k < 4:
                        total = total + v * v
                    else:
                        tail = tail + v * v
        total = total + jnp.where(ends, tail, 0.0)
        total = jnp.where(sub < 4, total, 0.0)
        return jnp.sum(total, axis=0, keepdims=True)

    def start_sums(slot, peers, got, order):
        for k in order:
            pltpu.make_async_remote_copy(
                src_ref=sums.at[slot, 0:1], dst_ref=got.at[k : k + 1], send_sem=sum_send.at[slot],
                recv_sem=sum_recv.at[slot], device_id=peers[k], device_id_type=MESH).start()

    def finish_sums(slot, peers, got):
        rows = got.at[0 : len(peers)]
        pltpu.make_async_copy(rows, rows, sum_recv.at[slot]).wait()
        total = sums[slot, 0:1] + jnp.sum(got[...], axis=0, keepdims=True)
        pltpu.make_async_copy(rows, rows, sum_send.at[slot]).wait()
        return total

    def in_one_row(parts):
        whole = jnp.sum(parts, axis=1, keepdims=True)
        return jnp.sum(jnp.where(lane // 32 == sub, whole, 0.0), axis=0, keepdims=True)

    def out_of_row(row):
        whole = jnp.sum(jnp.where(lane == 32 * sub, row, 0.0), axis=1, keepdims=True)
        return [jnp.broadcast_to(whole[n : n + 1], (1, LANES)) for n in range(4)]

    def greet(t):
        for stage in range(5):
            @pl.when(t == stage)
            def _(stage=stage):
                for side in range(2):
                    sign = (-1, 1)[side]
                    if stage > 0:
                        @pl.when(within(wide, sign * 2**stage, n_wide))
                        def _(side=side):
                            pl.semaphore_wait(greeting.at[stage - 1, side], 1)
                if stage < 4:
                    for side in range(2):
                        by = (-1, 1)[side] * 2 ** (stage + 1)

                        @pl.when(within(wide, by, n_wide))
                        def _(side=side, by=by):
                            pl.semaphore_signal(
                                greeting.at[stage, 1 - side], inc=1, device_id=(wide + by, cross),
                                device_id_type=MESH)

    points = gll_points()[0]
    here = jnp.where(sub < 4, 1.0, 0.0)

    def restrict(n):
        last = n == 4
        own_k = jnp.where(ends | last, 1.0, 0.0)
        own_j = jnp.where(last, keep_y, 0.0)
        own_i = here + jnp.where((sub == 4) & last, one_x, 0.0)
        columns = [column_ref[80 + 8 * i2 : 88 + 8 * i2] * own_i for i2 in range(2)]
        for c in range(3):
            lines = []
            for j in range(5):
                u = [held[n + 1, c * PER + j * 40 + k * 8 : c * PER + j * 40 + k * 8 + 8]
                     for k in range(5)]
                first, second = u[0], own_k * u[4]
                for k in range(1, 4):
                    part = float(points[k]) * u[k]
                    first, second = first + (u[k] - part), second + part
                lines.append((first, second))
            for k in range(2):
                first, second = lines[0][k], own_j * lines[4][k]
                for j in range(1, 4):
                    part = float(points[j]) * lines[j][k]
                    first, second = first + (lines[j][k] - part), second + part
                for j2, value in enumerate((first, second)):
                    for i2 in range(2):
                        row = j2 * 12 + i2 * 6 + c * 2 + k
                        rest[cross, n, row : row + 1] = jnp.sum(
                            value * columns[i2], axis=0, keepdims=True)
        for k in range(1, n_cross):
            z_copy(rest.at[cross, n], rest.at[cross, n], cz_send.at[n], cz_recv.at[n], k).start()

    def far_out(n):
        return lambda m: reach_out(
            coarse_out.at[n, 0:25], reach_in.at[n], cr_send.at[n], cr_recv.at[n], m)

    def far_back(n):
        return lambda m: reach_back(
            coarse_out.at[n, 0:25], reach_in.at[n], cr_send.at[n], cr_recv.at[n], m)

    def hand_on(n):
        for k in range(1, n_cross):
            z_copy(
                rest.at[from_z(k), n], rest.at[from_z(k), n], cz_send.at[n], cz_recv.at[n], k
            ).wait_recv()
        before = jnp.zeros((12, LANES), f32)
        for q in range(4):
            ahead = rest[q, n, 12:24]
            swapped = pltpu.roll(jnp.where(spread_to(low, 12), ahead, before), 64, 1)
            before = ahead
            value = rest[q, n, 0:12] + swapped
            moved = pltpu.roll(value, 1, 1)
            for i2 in range(2):
                for c in range(3):
                    first, last = i2 * 6 + c * 2, i2 * 6 + c * 2 + 1
                    row = i2 * 12 + q * 3 + c
                    coarse_out[n, row : row + 1] = value[first : first + 1] + jnp.where(
                        inner[:1], moved[last : last + 1], 0.0)
                    tails[row : row + 1] = value[last : last + 1]
        late = pltpu.roll(
            jnp.where(spread_to(ends, 24), tails[...], 0.0), 1, 1, stride=1, stride_axis=0)
        coarse_out[n, 24:25] = jnp.sum(late, axis=0, keepdims=True)
        each_reach(far_out(n), lambda c: c.start())
        for k in range(1, n_cross):
            z_copy(
                rest.at[cross, n], rest.at[cross, n], cz_send.at[n], cz_recv.at[n], k).wait_send()

    def elements_out():
        for k in range(1, n_cross):
            z_copy(elem_z.at[cross], elem_z.at[cross], ez_send, ez_recv, k).start()

    def elements_on():
        for k in range(1, n_cross):
            z_copy(elem_z.at[from_z(k)], elem_z.at[from_z(k)], ez_send, ez_recv, k).wait_recv()
        for q in range(4):
            for m in range(4):
                elem_out[m * 4 + q : m * 4 + q + 1] = elem_z[q, m : m + 1]
        each_reach(
            lambda m: reach_out(elem_out, elem_in, er_send, er_recv, m), lambda c: c.start())
        for k in range(1, n_cross):
            z_copy(elem_z.at[cross], elem_z.at[cross], ez_send, ez_recv, k).wait_send()

    def apply_all(base, squares, late=None):
        def step(t, carry):
            elements(t, t + 1)
            gather_local(t + 1)

            @pl.when(t == 0)
            def _():
                held[1] = load[...] - held[1]

            s = lax.rem(t + base, 2)
            exchange_start(t + 1, s)
            exchange_sent(1 - s)
            if squares:
                greet(t)
                norms[pl.ds(t, 1)] = square(t)

                @pl.when(t >= 1)
                def _():
                    restrict(t - 1)

                @pl.when(t == 1)
                def _():
                    elements_out()

                @pl.when(t >= 2)
                def _():
                    hand_on(t - 2)

                @pl.when(t == 3)
                def _():
                    elements_on()
            if late is not None:
                @pl.when(t == 3)
                def _():
                    late()
            exchange_finish(t + 1, s)
            return carry

        lax.fori_loop(0, 4, step, 0)

    exchange_start(0, 0)
    loads[5].wait()
    unpack(rhs_ref, load)
    exchange_finish(0, 0)
    apply_all(1, True)
    norms[4:5] = square(4)
    sums[0, 0:1] = in_one_row(norms[1:9])
    start_sums(0, z_peers, got_z, range(3))
    elements(4, 5)
    restrict(4)
    greet(4)
    restrict(3)
    hand_on(2)
    sums[1, 0:1] = finish_sums(0, z_peers, got_z)
    start_sums(1, w_peers, got_w.at[0], FAR_FIRST)
    hand_on(4)
    hand_on(3)

    each_reach(lambda m: reach_back(elem_out, elem_in, er_send, er_recv, m), lambda c: c.wait_recv())
    for m, by in enumerate(REACH):
        if by >= -HOME:
            elem_c[pl.ds(HOME + by, 16, stride=8)] = elem_in[m]
    elem_c[pl.ds(HOME, 16, stride=8)] = elem_out[...]
    for q in range(4):
        at = (12 + q) * 8
        elem_c[at : at + 8] = jnp.where(sub < 7, elem_c[at : at + 8], 0.0)
    each_reach(lambda m: reach_out(elem_out, elem_in, er_send, er_recv, m), lambda c: c.wait_send())

    for n in (0, 1, 2, 3, 4):
        each_reach(far_back(n), lambda c: c.wait_recv())
    largest = estimate(out_of_row(finish_sums(1, w_peers, got_w.at[0])))
    step_poly, rest_poly = smoothing(largest, FINE_RATIO)

    free = jnp.where(wide - HOME + sub < n_wide, 1.0, 0.0)
    for by in (0,) + REACH:
        part = None
        for n in range(5):
            source = coarse_out.at[n] if by == 0 else reach_in.at[n, REACH.index(by)]
            term = rest_poly[n] * source[0:25]
            part = term if part is None else part + term
        for i2 in range(2):
            s = HOME + by + i2
            if 0 <= s < 8:
                gather[pl.ds(i2 * 96 + s, 12, stride=8)] = part[i2 * 12 : i2 * 12 + 12]
                tail_in[i2 * 8 + s : i2 * 8 + s + 1] = part[24:25]
    for m in range(12):
        first = gather[m * 8 : m * 8 + 8] + gather[96 + m * 8 : 104 + m * 8]
        last = pltpu.roll(tail_in[0:8], 127 - m, 1) + pltpu.roll(tail_in[8:16], 115 - m, 1)
        vertex[0, m * 16 : m * 16 + 8] = first * free
        vertex[0, m * 16 + 8 : m * 16 + 16] = free * jnp.where(
            outer, pltpu.roll(first, 127, 1), last)

    def close(n, q):
        for c in range(3):
            at = (q * 6 + c * 2) * 8
            first, last = gather[pl.ds(at, 8)], gather[pl.ds(at + 8, 8)]
            first = first + jnp.where(inner, pltpu.roll(last, 1, 1), 0.0)
            vertex[n, pl.ds(at, 8)] = first * free
            vertex[n, pl.ds(at + 8, 8)] = free * jnp.where(outer, pltpu.roll(first, 127, 1), last)

    def close_all(n):
        for q in range(4):
            close(n, q)

    def coarse_step(n, carry):
        carried = {}

        def column(q):
            def at(c, k, up=0):
                return pl.ds((q + up) * 48 + c * 16 + k * 8, 8)

            def data(m):
                return elem_c[m * 32 + q * 8 : m * 32 + q * 8 + 8]

            fib = [data(0), data(1), data(2)]
            stiff = data(3)
            mass = jnp.where(stiff > 0.0, MASS_COEF, 0.0)
            modes = []
            for c in range(3):
                m = {}
                for k in range(2):
                    w = vertex[n, at(c, k), :]
                    beside = pltpu.roll(jnp.where(low, vertex[n, at(c, k, 1), :], w), 64, 1)
                    for b, v in enumerate((w + beside, beside - w)):
                        after = pltpu.roll(v, 7, 0)
                        m[0, b, k], m[1, b, k] = v + after, after - v
                modes.append({})
                for a in range(2):
                    for b in range(2):
                        first, last = m[a, b, 0], m[a, b, 1]
                        modes[c][a, b, 0], modes[c][a, b, 1] = first + last, last - first
            back = [{}, {}, {}]

            def put(c, mode, value):
                back[c][mode] = back[c][mode] + value if mode in back[c] else value

            for ones, weight in (((0, 0, 0), 16.0), ((1, 0, 0), 48.0), ((0, 1, 0), 48.0), ((0, 0, 1), 48.0)):
                at_mode = {
                    d: tuple(1 if d == e else ones[e] for e in range(3))
                    for d in range(3) if not ones[d]
                }
                grad = [
                    [modes[c][at_mode[d]] if d in at_mode else None for d in range(3)]
                    for c in range(3)
                ]
                part = stresses(grad, fib, stiff * (1.0 / weight))
                for d in at_mode:
                    for c in range(3):
                        put(c, at_mode[d], part[c, d])
            top = [modes[c][1, 1, 1] for c in range(3)]
            along = fib[0] * top[0] + fib[1] * top[1] + fib[2] * top[2]
            along = (stiff * (TOP_ALONG / 144.0)) * along
            top_scale = stiff * (TOP_SELF / 144.0)
            for c in range(3):
                put(c, (1, 1, 1), top_scale * top[c] + along * fib[c])
                for mode, value in modes[c].items():
                    count = sum(mode)
                    put(c, mode, (mass * (0.25 ** (3 - count) / 12.0**count)) * value)
                for k in range(2):
                    w = []
                    xs = {}
                    for a in range(2):
                        for b in range(2):
                            first, last = back[c][a, b, 0], back[c][a, b, 1]
                            xs[a, b] = first + last if k else first - last
                    for b in range(2):
                        w.append((xs[0, b] - xs[1, b]) + pltpu.roll(xs[0, b] + xs[1, b], 1, 0))
                    other = pltpu.roll(w[0] + w[1], 64, 1)
                    own = jnp.where(low, carried[c, k], other) if q else jnp.where(low, 0.0, other)
                    gather[at(c, k), :] = (w[0] - w[1]) + own
                    carried[c, k] = other

        for q in range(4):
            column(q)
        close_all(n + 1)
        return carry

    lax.fori_loop(0, 3, coarse_step, 0)

    def coarse_square(n):
        total = jnp.zeros((8, LANES), f32)
        tail = jnp.zeros((8, LANES), f32)
        for m in range(12):
            first, last = vertex[n, m * 16 : m * 16 + 8], vertex[n, m * 16 + 8 : m * 16 + 16]
            total = total + first * first
            tail = tail + last * last
        return (total + jnp.where(ends, tail, 0.0))[HOME : HOME + 1]

    for n in range(4):
        norms[n : n + 1] = coarse_square(n)
    sums[2, 0:1] = in_one_row(norms[0:8])
    start_sums(2, w_peers, got_w.at[1], FAR_FIRST)
    for n in range(5):
        each_reach(far_out(n), lambda c: c.wait_send())
    def add_steps(c, carry):
        at = pl.ds(pl.multiple_of(c * PER, 8), PER)
        value = held[0, at]
        for n in range(4):
            value = value + step_poly[n] * held[n + 1, at]
        held[0, at] = value
        return carry

    lax.fori_loop(0, 3, add_steps, 0)
    coarse_largest = estimate(out_of_row(finish_sums(2, w_peers, got_w.at[1])))
    coarse_poly, _ = smoothing(coarse_largest, COARSE_RATIO)
    left, right = column_ref[80:88], column_ref[88:96]
    for c in range(3):
        ends_k = []
        for k in range(2):
            w = []
            for up in range(2):
                at = pl.ds(pl.multiple_of((cross + up) * 48, 8) + (c * 16 + k * 8), 8)
                value = coarse_poly[0] * vertex[0, at]
                for n in range(1, 4):
                    value = value + coarse_poly[n] * vertex[n, at]
                w.append(value)
            ends_k.append((w[0], pltpu.roll(jnp.where(low, w[1], w[0]), 64, 1)))
        own = [ends_k[k][0][HOME : HOME + 1] for k in range(2)]
        for ey in range(2):
            a, b = own if ey == 0 else [pltpu.roll(v, 64, 1) for v in own]
            line = jnp.where(low[:1], a, pltpu.roll(b, 1, 1))
            cor_ref[c, 0, ey : ey + 1, :] = line[:, :65]
        nodes = []
        for k in range(2):
            first, last = [
                left * jnp.broadcast_to(v[HOME : HOME + 1], (8, LANES))
                + right * jnp.broadcast_to(v[HOME + 1 : HOME + 2], (8, LANES))
                for v in ends_k[k]
            ]
            step = last - first
            nodes.append(
                [first] + [first + float(points[j]) * step for j in range(1, 4)] + [last])
        for j in range(5):
            first, last = nodes[0][j], nodes[1][j]
            step = last - first
            for k in range(5):
                at = c * PER + j * 40 + k * 8
                more = first if k == 0 else last if k == 4 else first + float(points[k]) * step
                held[0, at : at + 8] = held[0, at : at + 8] + more

    row = lax.broadcasted_iota(jnp.int32, (256, 256), 0)
    z_at = lax.broadcasted_iota(jnp.int32, (256, 256), 1)
    spread = jnp.where(z_at == 4 * lax.rem(row, 64) + row // 64, 1.0, 0.0).astype(jnp.bfloat16)

    def to_nodes(value_at, ref):
        for c in range(3):
            for j in range(4):
                for k in range(5):
                    value = value_at(pl.ds(c * PER + j * 40 + k * 8, 8))
                    planes[k, pl.ds(c * 32 + j, 4, stride=8)] = value[:4]
                    planes[k, pl.ds(c * 32 + 4 + j, 4, stride=8)] = pltpu.roll(value, 64, 1)[:4]
        use = spread_to(low, 96)
        joined = jnp.concatenate(
            [jnp.where(use, planes[k], pltpu.roll(planes[k + 1], 64, 1)) for k in (0, 2)], 1)
        ref[:, :, :, 0:256] = selected(joined, spread).reshape(3, 4, 8, 256)
        ref[:, :, :, 256:257] = planes[4][:, 63:64].reshape(3, 4, 8, 1)

    def most(at):
        value = held[0, at]
        for n in range(3):
            value = value + step_poly[n] * held[n + 1, at]
        return value

    apply_all(1, False, lambda: to_nodes(most, out_ref))
    to_nodes(lambda at: step_poly[3] * held[4, at], last_ref)
    exchange_sent(0)


def on_device(rhs, start, stiffness, fibre_index):
    operands = [start, rhs, stiffness, fibre_index] + tables()
    vmem = pl.BlockSpec(memory_space=pltpu.VMEM)
    f32 = jnp.float32

    def room(*shape):
        return pltpu.VMEM(shape, f32)

    def flags(*shape):
        return pltpu.SemaphoreType.DMA(shape)

    most, last, correction = pl.pallas_call(
        kernel,
        out_shape=(
            jax.ShapeDtypeStruct(rhs.shape, f32),
            jax.ShapeDtypeStruct(rhs.shape, f32),
            jax.ShapeDtypeStruct((3, 1, 2, 65), f32),
        ),
        in_specs=[pl.BlockSpec(memory_space=pltpu.HBM)] * len(operands),
        out_specs=(vmem, vmem, vmem),
        scratch_shapes=[
            room(3, 4, 8, 257),
            room(3, 4, 8, 257),
            room(1, 2, 64),
            pltpu.VMEM((1, 2, 64), jnp.int32),
            room(PER, LANES),
            room(104, LANES),
            room(8, LANES),
            room(6, ROWS, LANES),
            room(ROWS, LANES),
            room(PER, LANES),
            room(ROWS, LANES),
            room(ROWS, LANES),
            room(ROWS, LANES),
            room(5, 96, LANES),
            room(2, 2, FACE_X, LANES),
            room(2, 2, FACE_Y, LANES),
            room(2, 4, EDGE, LANES),
            room(2, 2, FACE_X, LANES),
            room(2, 2, FACE_Y, LANES),
            room(2, 4, EDGE, LANES),
            room(4, 5, 24, LANES),
            room(5, 32, LANES),
            room(24, LANES),
            room(16, LANES),
            room(5, 8, 25, LANES),
            room(4, 8, LANES),
            room(16, LANES),
            room(8, 16, LANES),
            room(128, LANES),
            room(4, 240, LANES),
            room(240, LANES),
            room(3, 8, LANES),
            room(16, LANES),
            room(8, LANES),
            room(2, 32, LANES),
            flags(2, 8), flags(2, 8),
            flags(3), flags(3),
            flags(3), flags(3),
            flags(5, 3), flags(5, 3),
            flags(8), flags(8),
            flags(5, 8), flags(5, 8),
            flags(6),
            pltpu.SemaphoreType.REGULAR((4, 2)),
        ],
        compiler_params=pltpu.CompilerParams(
            collective_id=0, has_side_effects=True, vmem_limit_bytes=60 * 1024 * 1024
        ),
    )(*operands)
    return most + last, correction


def solution(mesh):
    in_specs = (
        P(None, "wide", "cross", None),
        P(None, "wide", "cross", None),
        P("wide", "cross", None),
        P("wide", "cross", None),
    )
    out_specs = (P(None, "wide", "cross", None), P(None, "wide", "cross", None))
    return jax.shard_map(
        on_device, mesh=mesh, in_specs=in_specs, out_specs=out_specs, check_vma=False
    )
```
